256 devices in a mesh: gx: 8 (over x, y_lo), gy: 32 (over y_hi, z, core).
Axes of the slice: x: 4, y: 4 (y_hi: 2, y_lo: 2; y = y_hi * 2 + y_lo), z: 8, core: 2. Of those that a mesh axis runs over, the one named last changes fastest.
Arguments:
- positions: float32 [3, 8, 32, 2940], P(None, 'gx', 'gy'), may hold values from 0 to 480, as said below
- species: int32 [8, 32, 2940], P('gx', 'gy'), may hold values from 0 to 4
- mig_rows: int32 [8, 32, 8, 64], P('gx', 'gy'), may hold values from 0 to 2940, as said below
- ghost_rows: int32 [8, 32, 8, 1260], P('gx', 'gy'), may hold values from 0 to 3452, as said below
- edge_center: int32 [8, 32, 512], P('gx', 'gy'), may hold values from 0 to 2939, as said below
- edge_neighbor: int32 [8, 32, 512], P('gx', 'gy'), may hold values from 0 to 13531, as said below
- edge_blocks: int32 [8, 32], P('gx', 'gy'), may hold values from 1 to 4, as said below
- w_radial: float32 [8, 256], replicated, may hold values from -2 to 2
- w_kind_center: float32 [4, 256], replicated, may hold values from -4 to 4
- w_kind_neigh: float32 [4, 256], replicated, may hold values from -4 to 4
- w_two: bfloat16 [256, 256], replicated, may hold values from -0.375 to 0.375
- w_edge: bfloat16 [2, 256, 192], replicated, may hold values from -1.5 to 1.5
- w_env: bfloat16 [2, 256, 192], replicated, may hold values from -1.5 to 1.5
- w_update: bfloat16 [2, 448, 256], replicated, may hold values from -0.25 to 0.25
- w_out: bfloat16 [256], replicated, may hold values from -0.375 to 0.375
Outputs:
- owned_positions: float32 [3, 8, 32, 3452], P(None, 'gx', 'gy')
- forces: float32 [3, 8, 32, 3452], P(None, 'gx', 'gy')
- atom_energy: float32 [8, 32, 3452], P('gx', 'gy')
The draws below stay inside these ranges and needn't reach their ends.
Inputs may be any that keep to these rules, and one draw needn't show every extreme that they name: `mig_rows`: each domain's lists name its own slots, each at most once over all eight directions; the value 2940 marks an empty entry and is in every list; no list points off the grid. `ghost_rows`: slots after migration, distinct within a direction; the value 3452 marks an empty entry. `edge_center`: slots of the domain's atoms before migration. `edge_neighbor`: never equal to the edge's center; a slot of the extended list. `edge_blocks`: edges of blocks at or beyond this count are padding; some domain has all 4 blocks live. `positions`: x lies in the domain's column of width 15, y in its row of width 15, z between 0 and 15 * 60 / 7.
All inputs are finite; a program needn't handle non-finite values.
Results may differ from the reference program's by a relative error of at most 0.015.
Values sent between devices are 32-bit elements; how exact they have to be, the bound alone decides.
No kernel may reach another device: no remote copies, remote signals or barrier semaphores. Data moves between devices by JAX's collectives and lax.ppermute only.
A program may use at most 64 MiB of HBM per device.

```python
import math
import jax
import jax.numpy as jnp
from jax import lax

ZL = 60
SIDE = 7
MCAP = 64
E_DEV = 512
LAT = 256
C = 64
NRAD = 8
NSPEC = 4
LAYERS = 2
DOM_X = 8
DOM_Y = 32
A_DEV = 2940
GCAP = 1260
A_OWN = 3452
A_EXT = 13532
NBLK = 4


STEP_X = (-1, -1, -1, 0, 0, 1, 1, 1)


STEP_Y = (-1, 0, 1, -1, 1, -1, 0, 1)


def lattice_of():
    slot_ids = jnp.arange(A_DEV, dtype=jnp.int32)
    return (slot_ids, slot_ids % SIDE, slot_ids // SIDE % SIDE, slot_ids // (SIDE * SIDE))


def outer_sign(coord):
    return (coord == SIDE - 1).astype(jnp.int32) - (coord == 0).astype(jnp.int32)


def in_band(coord, step):
    return jnp.where(step < 0, coord <= 2, jnp.where(step > 0, coord >= SIDE - 3, True))


def migration(key):
    key_order, key_fill = jax.random.split(jax.random.fold_in(key, 11))
    slot_ids, along_x, along_y, along_z = lattice_of()
    steps_x = jnp.array(STEP_X, jnp.int32)
    steps_y = jnp.array(STEP_Y, jnp.int32)
    region = (outer_sign(along_x)[None, :] == steps_x[:, None]) & (outer_sign(along_y)[None, :] == steps_y[:, None])
    members = jnp.sum(region.astype(jnp.int32), 1)
    bound = (1 << 30) // A_DEV - 1
    scores = jax.random.randint(key_order, (DOM_X, DOM_Y, 8, A_DEV), 0, bound) * A_DEV + slot_ids
    scores = jnp.where(region[None, None], scores, bound * A_DEV + slot_ids)
    order = jnp.argsort(scores, axis=3)[..., :MCAP].astype(jnp.int32)
    fills = jax.random.randint(key_fill, (DOM_X, DOM_Y, 8, 1), MCAP // 2, MCAP)
    fills = jnp.minimum(fills, members[None, None, :, None])
    col = jnp.arange(DOM_X, dtype=jnp.int32)[:, None, None, None] + steps_x[None, None, :, None]
    row = jnp.arange(DOM_Y, dtype=jnp.int32)[None, :, None, None] + steps_y[None, None, :, None]
    inside = (col >= 0) & (col < DOM_X) & (row >= 0) & (row < DOM_Y)
    place = jnp.arange(MCAP, dtype=jnp.int32)[None, None, None, :]
    return jnp.where((place < fills) & inside, order, A_DEV).astype(jnp.int32)


def layout(key):
    leaving = migration(key)
    slot_ids, along_x, along_y, along_z = lattice_of()
    grid_x = jnp.arange(DOM_X, dtype=jnp.int32)[:, None, None]
    grid_y = jnp.arange(DOM_Y, dtype=jnp.int32)[None, :, None]
    flat_leave = leaving.reshape(DOM_X, DOM_Y, 8 * MCAP)
    entry = jnp.broadcast_to(jnp.arange(8 * MCAP, dtype=jnp.int32)[None, None, :], flat_leave.shape)
    dest_dir = jnp.full((DOM_X, DOM_Y, A_DEV + 1), 8, jnp.int32).at[grid_x, grid_y, flat_leave].set(entry // MCAP)[..., :A_DEV]
    dest_pos = jnp.zeros((DOM_X, DOM_Y, A_DEV + 1), jnp.int32).at[grid_x, grid_y, flat_leave].set(entry % MCAP)[..., :A_DEV]
    moved = dest_dir < 8
    steps_x = jnp.array(STEP_X, jnp.int32)
    steps_y = jnp.array(STEP_Y, jnp.int32)
    send_x = jnp.arange(DOM_X, dtype=jnp.int32)[:, None, None, None] + steps_x[None, None, :, None]
    send_y = jnp.arange(DOM_Y, dtype=jnp.int32)[None, :, None, None] + steps_y[None, None, :, None]
    inside = (send_x >= 0) & (send_x < DOM_X) & (send_y >= 0) & (send_y < DOM_Y)
    back_dir = (7 - jnp.arange(8, dtype=jnp.int32))[None, None, :, None]
    place = jnp.arange(MCAP, dtype=jnp.int32)[None, None, None, :]
    arrived = leaving[jnp.clip(send_x, 0, DOM_X - 1), jnp.clip(send_y, 0, DOM_Y - 1), back_dir, place]
    arrived = jnp.where(inside, arrived, A_DEV)
    arrive_x = (arrived % SIDE + steps_x[None, None, :, None] * SIDE).reshape(DOM_X, DOM_Y, 8 * MCAP)
    arrive_y = (arrived // SIDE % SIDE + steps_y[None, None, :, None] * SIDE).reshape(DOM_X, DOM_Y, 8 * MCAP)
    present = (arrived < A_DEV).reshape(DOM_X, DOM_Y, 8 * MCAP)
    band_own = in_band(along_x[None, :], steps_x[:, None]) & in_band(along_y[None, :], steps_y[:, None])
    chosen_own = band_own[None, None] & jnp.logical_not(moved)[:, :, None, :]
    band_new = in_band(arrive_x[:, :, None, :], steps_x[None, None, :, None]) & in_band(arrive_y[:, :, None, :], steps_y[None, None, :, None])
    chosen_new = band_new & present[:, :, None, :]
    rank_new = jnp.cumsum(chosen_new.astype(jnp.int32), axis=3) - 1
    count_new = jnp.sum(chosen_new.astype(jnp.int32), axis=3, keepdims=True)
    rank_own = count_new + jnp.cumsum(chosen_own.astype(jnp.int32), axis=3) - 1
    chosen = jnp.concatenate([chosen_own, chosen_new], 3)
    rank = jnp.concatenate([rank_own, rank_new], 3).astype(jnp.int32)
    listed = chosen & (rank < GCAP)
    return (dest_dir, dest_pos, listed, rank)


def draw_positions(key, part):
    key = jax.random.fold_in(key, 1)
    key_x, key_y, key_z = jax.random.split(key, 3)
    shape = (DOM_X, DOM_Y, A_DEV)
    slot_ids, along_x, along_y, along_z = lattice_of()
    spacing = 15.0 / SIDE
    col = jnp.arange(DOM_X, dtype=jnp.float32)[:, None, None] * SIDE
    row = jnp.arange(DOM_Y, dtype=jnp.float32)[None, :, None] * SIDE
    draw_x = jax.random.uniform(key_x, shape)
    draw_y = jax.random.uniform(key_y, shape)
    draw_z = jax.random.uniform(key_z, shape)
    shift_x = 0.6 * draw_x - 0.3
    shift_y = 0.6 * draw_y - 0.3
    shift_z = 0.6 * draw_z - 0.3
    coord_x = (col + along_x.astype(jnp.float32) + 0.5 + shift_x) * spacing
    coord_y = (row + along_y.astype(jnp.float32) + 0.5 + shift_y) * spacing
    coord_z = (along_z.astype(jnp.float32) + 0.5 + shift_z) * spacing
    return jnp.stack([coord_x, coord_y, coord_z], 0).astype(jnp.float32)


def draw_mig_rows(key, part):
    return migration(key)


def draw_ghost_rows(key, part):
    dest_dir, dest_pos, listed, rank = layout(key)
    slot_ids = jnp.arange(A_OWN, dtype=jnp.int32)
    index_x = jnp.broadcast_to(jnp.arange(DOM_X, dtype=jnp.int32)[:, None, None, None], listed.shape)
    index_y = jnp.broadcast_to(jnp.arange(DOM_Y, dtype=jnp.int32)[None, :, None, None], listed.shape)
    index_k = jnp.broadcast_to(jnp.arange(8, dtype=jnp.int32)[None, None, :, None], listed.shape)
    place = jnp.where(listed, rank, GCAP)
    values = jnp.broadcast_to(slot_ids[None, None, None, :], listed.shape)
    table = jnp.full((DOM_X, DOM_Y, 8, GCAP + 1), A_OWN, jnp.int32)
    table = table.at[index_x, index_y, index_k, place].set(values)
    return table[..., :GCAP].astype(jnp.int32)


def edge_pairs(key):
    dest_dir, dest_pos, listed, rank = layout(key)
    key_edges = jax.random.fold_in(key, 13)
    key_c, key_xy, key_z = jax.random.split(key_edges, 3)
    shape = (DOM_X, DOM_Y, E_DEV)
    center = jax.random.randint(key_c, shape, 0, A_DEV).astype(jnp.int32)
    offset = jax.random.randint(key_xy, shape, 0, 36)
    close = offset < 24
    inner = offset + (offset >= 12).astype(jnp.int32)
    outer = jnp.clip(offset - 24, 0, 11)
    reach_far = 3 * (2 * (outer // 3 % 2) - 1)
    lateral = outer % 3 - 1
    along_first = outer < 6
    move_x = jnp.where(close, inner // 5 - 2, jnp.where(along_first, reach_far, lateral))
    move_y = jnp.where(close, inner % 5 - 2, jnp.where(along_first, lateral, reach_far))
    move_z = jnp.where(close, jax.random.randint(key_z, shape, -2, 3), 0)
    along_x = center % SIDE
    along_y = center // SIDE % SIDE
    along_z = center // (SIDE * SIDE)
    grid_x = jnp.arange(DOM_X, dtype=jnp.int32)[:, None, None]
    grid_y = jnp.arange(DOM_Y, dtype=jnp.int32)[None, :, None]
    reach_x = along_x + move_x
    move_x = jnp.where((grid_x == 0) & (reach_x < 0) | (grid_x == DOM_X - 1) & (reach_x > SIDE - 1), -move_x, move_x)
    reach_x = along_x + move_x
    reach_y = along_y + move_y
    move_y = jnp.where((grid_y == 0) & (reach_y < 0) | (grid_y == DOM_Y - 1) & (reach_y > SIDE - 1), -move_y, move_y)
    reach_y = along_y + move_y
    reach_z = jnp.clip(along_z + move_z, 0, ZL - 1)
    hop_x = (reach_x > SIDE - 1).astype(jnp.int32) - (reach_x < 0).astype(jnp.int32)
    hop_y = (reach_y > SIDE - 1).astype(jnp.int32) - (reach_y < 0).astype(jnp.int32)
    target = reach_x - hop_x * SIDE + SIDE * (reach_y - hop_y * SIDE) + SIDE * SIDE * reach_z
    direction = (hop_x + 1) * 3 + hop_y + 1
    direction = direction - (direction > 4).astype(jnp.int32)
    at_home = (hop_x == 0) & (hop_y == 0)
    safe_dir = jnp.clip(direction, 0, 7)
    opposite = 7 - safe_dir
    steps_x = jnp.array(STEP_X, jnp.int32)
    steps_y = jnp.array(STEP_Y, jnp.int32)
    home_dir_raw = dest_dir[grid_x, grid_y, target]
    home_moved = home_dir_raw < 8
    home_dir = jnp.clip(home_dir_raw, 0, 7)
    owner_x = jnp.clip(grid_x + steps_x[home_dir], 0, DOM_X - 1)
    owner_y = jnp.clip(grid_y + steps_y[home_dir], 0, DOM_Y - 1)
    owner_slot = A_DEV + (7 - home_dir) * MCAP + dest_pos[grid_x, grid_y, target]
    owner_rank = rank[owner_x, owner_y, 7 - home_dir, owner_slot]
    home_value = jnp.where(home_moved, A_OWN + home_dir * GCAP + owner_rank, target)
    other_x = jnp.clip(grid_x + hop_x, 0, DOM_X - 1)
    other_y = jnp.clip(grid_y + hop_y, 0, DOM_Y - 1)
    listed_there = listed[other_x, other_y, opposite, target]
    rank_there = rank[other_x, other_y, opposite, target]
    came_here = dest_dir[other_x, other_y, target] == opposite
    arrival_slot = A_DEV + safe_dir * MCAP + dest_pos[other_x, other_y, target]
    away_value = jnp.where(listed_there, A_OWN + safe_dir * GCAP + rank_there, jnp.where(came_here, arrival_slot, A_OWN + safe_dir * GCAP + GCAP - 1))
    neighbor = jnp.where(at_home, home_value, away_value)
    return (center, neighbor.astype(jnp.int32))


def draw_edge_center(key, part):
    return edge_pairs(key)[0]


def draw_edge_neighbor(key, part):
    return edge_pairs(key)[1]


def draw_edge_blocks(key, part):
    key = jax.random.fold_in(key, 5)
    key_a, key_b = jax.random.split(key)
    full = jax.random.randint(key_a, (DOM_X, DOM_Y), 0, 4) == 0
    some = jax.random.randint(key_b, (DOM_X, DOM_Y), 1, NBLK // 2 + 1)
    blocks = jnp.where(full, NBLK, some)
    return blocks.at[0, 0].set(NBLK).astype(jnp.int32)


def set_ends(drawn, key, low, high):
    spot = [jax.random.randint(jax.random.fold_in(key, axis), (), 0, length) for axis, length in enumerate(drawn.shape)]
    main_axis = drawn.shape.index(max(drawn.shape))
    beside = spot[:main_axis] + [(spot[main_axis] + 1) % drawn.shape[main_axis]] + spot[main_axis + 1:]
    return drawn.at[tuple(spot)].set(low).at[tuple(beside)].set(high)


def centred(key, shape, width, limit, held_as=jnp.bfloat16):
    return jnp.clip(width * jax.random.normal(key, shape, jnp.float32), -limit, limit).astype(held_as)


def setup_inputs(seed: int = 0) -> dict:
    streams_of = jax.random.split(jax.random.key(seed), 16)
    positions = draw_positions(jax.random.fold_in(streams_of[15], 71), 0)
    species = set_ends(jax.random.randint(streams_of[1], (DOM_X, DOM_Y, A_DEV), 0, NSPEC + 1), jax.random.fold_in(streams_of[1], 1), 0, NSPEC).astype(jnp.int32)
    mig_rows = draw_mig_rows(jax.random.fold_in(streams_of[15], 71), 0)
    ghost_rows = draw_ghost_rows(jax.random.fold_in(streams_of[15], 71), 0)
    edge_center = draw_edge_center(jax.random.fold_in(streams_of[15], 71), 0)
    edge_neighbor = draw_edge_neighbor(jax.random.fold_in(streams_of[15], 71), 0)
    edge_blocks = draw_edge_blocks(jax.random.fold_in(streams_of[15], 71), 0)
    w_radial = centred(streams_of[7], (NRAD, LAT), NRAD ** -0.5, 2.0, jnp.float32)
    w_kind_center = centred(streams_of[8], (NSPEC, LAT), 0.6, 4.0, jnp.float32)
    w_kind_neigh = centred(streams_of[9], (NSPEC, LAT), 0.6, 4.0, jnp.float32)
    w_two = centred(streams_of[10], (LAT, LAT), LAT ** -0.5, 0.375)
    w_edge = centred(streams_of[11], (LAYERS, LAT, 3 * C), (LAT // 16) ** -0.5, 1.5)
    w_env = centred(streams_of[12], (LAYERS, LAT, 3 * C), (LAT // 16) ** -0.5, 1.5)
    w_update = centred(streams_of[13], (LAYERS, LAT + 3 * C, LAT), (LAT + 3 * C) ** -0.5, 0.25)
    w_out = centred(streams_of[14], (LAT,), LAT ** -0.5, 0.375)
    return dict(positions=positions, species=species, mig_rows=mig_rows, ghost_rows=ghost_rows, edge_center=edge_center, edge_neighbor=edge_neighbor, edge_blocks=edge_blocks, w_radial=w_radial, w_kind_center=w_kind_center, w_kind_neigh=w_kind_neigh, w_two=w_two, w_edge=w_edge, w_env=w_env, w_update=w_update, w_out=w_out)


DIRS = ((-1, -1), (-1, 0), (-1, 1), (0, -1), (0, 1), (1, -1), (1, 0), (1, 1))
DEGREE_OF = (0, 1, 1, 1, 2, 2, 2, 2, 2)
CUTOFF = 6.0
SOFTENING = 0.01
BASIS_WIDTH = 0.8
ENV_SCALE = 0.3

def harmonics(unit):
    ux, uy, uz = (unit[0], unit[1], unit[2])
    square = ux * ux + uy * uy + uz * uz
    root3 = math.sqrt(3.0)
    root15 = math.sqrt(15.0)
    cols = [jnp.ones_like(ux), root3 * ux, root3 * uy, root3 * uz, root15 * ux * uy, root15 * uy * uz, root15 * ux * uz, 0.5 * math.sqrt(5.0) * (3.0 * uz * uz - square), 0.5 * root15 * (ux * ux - uy * uy)]
    return jnp.stack(cols, 1)

def local_energy(ext_pos, ext_kind, center, neighbor, live_blocks, n_own, w_radial, w_kind_center, w_kind_neigh, w_two, w_edge, w_env, w_update, w_out):
    edges = center.shape[0]
    chans = w_edge.shape[2] // 3
    nspec = w_kind_center.shape[0]
    nrad = w_radial.shape[0]
    delta = ext_pos[:, neighbor] - ext_pos[:, center]
    radius = jnp.sqrt(lax.optimization_barrier(jnp.sum(delta * delta, 0)) + SOFTENING)
    kind_c = ext_kind[center]
    kind_n = ext_kind[neighbor]
    block_live = jnp.arange(edges, dtype=jnp.int32) // 128 < live_blocks
    live = block_live.astype(jnp.float32) * (kind_c > 0.5).astype(jnp.float32) * (kind_n > 0.5).astype(jnp.float32)
    envelope = live * jnp.square(jnp.maximum(0.0, 1.0 - radius * radius / (CUTOFF * CUTOFF)))
    sph = harmonics(delta / CUTOFF)
    centers_mu = jnp.arange(nrad, dtype=jnp.float32) * (CUTOFF / (nrad - 1))
    radial = jnp.exp(-jnp.square((radius[:, None] - centers_mu[None, :]) / BASIS_WIDTH))
    ids = jnp.arange(1, nspec + 1, dtype=jnp.float32)
    onehot_c = (kind_c[:, None] == ids[None, :]).astype(jnp.float32)
    onehot_n = (kind_n[:, None] == ids[None, :]).astype(jnp.float32)
    high = lax.Precision.HIGHEST
    pre = jnp.dot(radial, w_radial, precision=high) + jnp.dot(onehot_c, w_kind_center, precision=high) + jnp.dot(onehot_n, w_kind_neigh, precision=high)
    hidden = jax.nn.silu(pre).astype(jnp.bfloat16)
    latent = jax.nn.silu(jnp.dot(hidden, w_two, preferred_element_type=jnp.float32)) * envelope[:, None]
    for layer in range(w_edge.shape[0]):
        latent_b = latent.astype(jnp.bfloat16)
        edge_mix = jnp.dot(latent_b, w_edge[layer], preferred_element_type=jnp.float32)
        env_mix = jnp.dot(latent_b, w_env[layer], preferred_element_type=jnp.float32)
        terms = jnp.concatenate([env_mix[:, DEGREE_OF[comp] * chans:(DEGREE_OF[comp] + 1) * chans] * sph[:, comp:comp + 1] for comp in range(9)], 1)
        environment = jnp.zeros((n_own, 9 * chans), jnp.float32).at[center].add(terms) * ENV_SCALE
        env_at = environment[center]
        groups = []
        for degree, (first, last) in enumerate(((0, 1), (1, 4), (4, 9))):
            weight_l = edge_mix[:, degree * chans:(degree + 1) * chans]
            acc = jnp.zeros((edges, chans), jnp.float32)
            for comp in range(first, last):
                acc = acc + weight_l * sph[:, comp:comp + 1] * env_at[:, comp * chans:(comp + 1) * chans]
            groups.append(acc)
        invariants = jnp.concatenate(groups, 1).astype(jnp.bfloat16)
        joined = jnp.concatenate([latent_b, invariants], 1)
        update = jnp.dot(joined, w_update[layer], preferred_element_type=jnp.float32)
        latent = latent + jax.nn.silu(update) * envelope[:, None]
    edge_energy = envelope * jnp.dot(latent.astype(jnp.bfloat16), w_out, preferred_element_type=jnp.float32)
    atoms = jnp.zeros((n_own,), jnp.float32).at[center].add(edge_energy)
    return (jnp.sum(edge_energy), atoms)

def grid_from(table, step_x, step_y):
    widths = [(0, 0), (1, 1), (1, 1)] + [(0, 0)] * (table.ndim - 3)
    padded = jnp.pad(table, widths)
    return padded[:, 1 + step_x:1 + step_x + DOM_X, 1 + step_y:1 + step_y + DOM_Y]

def pick_rows(table, rows):
    flat = rows.reshape(DOM_X, DOM_Y, -1)
    got = jnp.take_along_axis(table, jnp.broadcast_to(flat[None], (table.shape[0],) + flat.shape), axis=3)
    return got.reshape(table.shape[:3] + rows.shape[2:])

def receive(sent):
    blocks = [grid_from(sent[:, :, :, 7 - index], DIRS[index][0], DIRS[index][1]) for index in range(8)]
    return jnp.concatenate(blocks, 3)

def reference(positions, species, mig_rows, ghost_rows, edge_center, edge_neighbor, edge_blocks, w_radial, w_kind_center, w_kind_neigh, w_two, w_edge, w_env, w_update, w_out):
    grid_x = jnp.arange(DOM_X, dtype=jnp.int32)[:, None, None]
    grid_y = jnp.arange(DOM_Y, dtype=jnp.int32)[None, :, None]
    payload = jnp.concatenate([positions, species.astype(jnp.float32)[None]], 0)
    padded = jnp.concatenate([payload, jnp.zeros((4, DOM_X, DOM_Y, 1), jnp.float32)], 3)
    sent = pick_rows(padded, mig_rows)
    keep = jnp.ones((DOM_X, DOM_Y, A_DEV + 1), jnp.float32).at[grid_x, grid_y, mig_rows.reshape(DOM_X, DOM_Y, -1)].set(0.0)
    owned = jnp.concatenate([payload * keep[None, :, :, :A_DEV], receive(sent)], 3)
    owned_pad = jnp.concatenate([owned, jnp.zeros((4, DOM_X, DOM_Y, 1), jnp.float32)], 3)
    extended = jnp.concatenate([owned, receive(pick_rows(owned_pad, ghost_rows))], 3)
    count = DOM_X * DOM_Y
    ext_flat = jnp.transpose(extended.reshape(4, count, A_EXT), (1, 0, 2))
    centers = edge_center.reshape(count, E_DEV)
    neighbors = edge_neighbor.reshape(count, E_DEV)
    blocks = edge_blocks.reshape(count)

    def one_domain(item):
        ext_one, center, neighbor, live_blocks = item

        def energy_of(coords):
            return local_energy(coords, ext_one[3], center, neighbor, live_blocks, A_OWN, w_radial, w_kind_center, w_kind_neigh, w_two, w_edge, w_env, w_update, w_out)
        total, pullback, atoms = jax.vjp(energy_of, ext_one[:3], has_aux=True)
        return (pullback(jnp.ones_like(total))[0], atoms)
    grads, atoms = lax.map(one_domain, (ext_flat, centers, neighbors, blocks))
    grads = jnp.transpose(grads, (1, 0, 2)).reshape(3, DOM_X, DOM_Y, A_EXT)
    own_grad = grads[..., :A_OWN]
    ghost_grad = grads[..., A_OWN:].reshape(3, DOM_X, DOM_Y, 8, GCAP)
    returned = receive(ghost_grad)
    total = jnp.concatenate([own_grad, jnp.zeros((3, DOM_X, DOM_Y, 1), jnp.float32)], 3)
    total = total.at[:, grid_x, grid_y, ghost_rows.reshape(DOM_X, DOM_Y, -1)].add(returned)
    forces = -total[..., :A_OWN]
    atom_energy = atoms.reshape(DOM_X, DOM_Y, A_OWN)
    return (owned[:3], forces, atom_energy)
```

```python
import math

import jax
import jax.numpy as jnp
from jax import lax
from jax.experimental import pallas as pl
from jax.experimental.pallas import tpu as pltpu
from jax.sharding import PartitionSpec as P

CUTOFF = 6.0
SOFTENING = 0.01
BASIS_WIDTH = 0.8
ENV_SCALE = 0.3
ROOT3 = math.sqrt(3.0)
ROOT5 = math.sqrt(5.0)
ROOT15 = math.sqrt(15.0)
DIRS = ((-1, -1), (-1, 0), (-1, 1), (0, -1), (0, 1), (1, -1), (1, 0), (1, 1))
SLOTS = 2940
MOVES = 64
OWNED = 3452
GHOSTS = 1260
EDGES = 512
LANES = 128
KEPT_ROWS = 23
F32 = jnp.float32
BF16 = jnp.bfloat16
VMEM_LIMIT = 48 * 1024 * 1024

NN = (((1,), (0,)), ((), ()))
NT = (((1,), (1,)), ((), ()))
TN = (((0,), (0,)), ((), ()))


def mm(a, b, dims=NN):
    return lax.dot_general(a, b, dims, preferred_element_type=F32)


def mm_high(a, b, dims=NN):
    return lax.dot_general(
        a, b, dims, precision=lax.Precision.HIGHEST, preferred_element_type=F32
    )


def split(x):
    top = x.astype(BF16)
    return top, (x - top.astype(F32)).astype(BF16)


def lane_pick(row, low):
    table = jnp.broadcast_to(row, low.shape)
    return jnp.take_along_axis(table, low, axis=1, mode="promise_in_bounds")


def full_row(ref, lead, start, size):
    stop = min(start + LANES, size)
    piece = ref[lead + (slice(None), slice(start, stop))]
    if stop - start < LANES:
        pad = jnp.zeros((1, LANES - (stop - start)), piece.dtype)
        piece = jnp.concatenate([piece, pad], axis=1)
    return piece


def payload_row(pos_ref, kind_ref, chan, h):
    if chan < 3:
        return full_row(pos_ref, (chan,), h * LANES, SLOTS)
    return full_row(kind_ref, (), h * LANES, SLOTS).astype(F32)


def send_kernel(pos_ref, kind_ref, mig_ref, nbr_ref, msg_ref):
    rows = mig_ref[...]
    rows = jnp.concatenate([rows, jnp.full((8, LANES - MOVES), -1, jnp.int32)], axis=1)
    high, low = rows >> 7, rows & 127
    picked = [jnp.zeros((8, LANES), F32) for _ in range(4)]
    for h in range(KEPT_ROWS):
        here = high == h
        for c in range(4):
            got = lane_pick(payload_row(pos_ref, kind_ref, c, h), low)
            picked[c] = jnp.where(here, got, picked[c])
    for p in range(2):
        msg_ref[pl.ds(8 * p, 8), :] = picked[2 * p] + pltpu.roll(picked[2 * p + 1], MOVES, 1)
    for r in range(4):
        msg_ref[pl.ds(16 + r, 1), :] = nbr_ref[:, r * LANES : (r + 1) * LANES].astype(F32)
    msg_ref[pl.ds(20, 4), :] = jnp.zeros((4, LANES), F32)


def keep_kernel(pos_ref, kind_ref, mig_ref, kept_ref):
    rows = mig_ref[...]
    rows = jnp.concatenate([rows, jnp.full((8, LANES - MOVES), -1, jnp.int32)], axis=1)
    high, low = rows >> 7, rows & 127
    sub32 = lax.broadcasted_iota(jnp.int32, (32, LANES), 0)
    sub128 = lax.broadcasted_iota(jnp.int32, (LANES, LANES), 0)
    left = jnp.zeros((32, LANES), F32)
    for k in range(8):
        a = (sub32 == high[k : k + 1, :]).astype(F32).astype(BF16)
        b = (sub128 == low[k : k + 1, :]).astype(F32).astype(BF16)
        left = left + mm(a, b, NT)
    stay = left < 0.5
    for c in range(4):
        table = jnp.concatenate(
            [payload_row(pos_ref, kind_ref, c, h) for h in range(KEPT_ROWS)]
            + [jnp.zeros((1, LANES), F32)],
            axis=0,
        )
        kept_ref[c] = jnp.where(stay[:24, :], table, 0.0)


def answer_kernel(
    grid, where_ref, own_ref, below_ref, above_ref, ghost_ref, center_ref, kept_ref,
    left_ref, right_ref, same_ref, center_out, slot_ref, arrive_ref,
):
    nx, ny = grid
    ix, iy = where_ref[0], where_ref[1]
    by_dy = {-1: below_ref, 0: own_ref, 1: above_ref}
    inside = []
    for dx, dy in DIRS:
        ok = (ix + dx >= 0) & (ix + dx < nx) & (iy + dy >= 0) & (iy + dy < ny)
        inside.append(ok.astype(jnp.int32))
    for p in range(2):
        for k, (dx, dy) in enumerate(DIRS):
            row = by_dy[dy][dx + 1, pl.ds(8 * p + 7 - k, 1), :]
            arrive_ref[p, pl.ds(k, 1), :] = row * inside[k].astype(F32)
    groups = []
    for o in range(0, 8, 2):
        parts = []
        for d in (o, o + 1):
            dx, dy = DIRS[d]
            listed = by_dy[dy][dx + 1, pl.ds(16, 4), :].astype(jnp.int32)
            rank = listed - (OWNED + GHOSTS * (7 - d))
            ok = (rank >= 0) & (rank < GHOSTS) & (inside[d] > 0)
            parts.append(jnp.where(ok, rank, -1))
        rank = jnp.concatenate(parts, axis=0)
        high, low = rank >> 7, rank & 127
        slot = jnp.full((8, LANES), -1, jnp.int32)
        upper = lax.broadcasted_iota(jnp.int32, (8, LANES), 0) < 4
        for h in range(10):
            stop = min((h + 1) * LANES, GHOSTS)
            pair = []
            for d in (o, o + 1):
                row = ghost_ref[pl.ds(d, 1), h * LANES : stop]
                if stop - h * LANES < LANES:
                    pad = jnp.full((1, LANES - (stop - h * LANES)), -1, jnp.int32)
                    row = jnp.concatenate([row, pad], axis=1)
                pair.append(jnp.broadcast_to(row, (8, LANES)))
            table = jnp.where(upper, pair[0], pair[1])
            got = jnp.take_along_axis(table, low, axis=1, mode="promise_in_bounds")
            slot = jnp.where(high == h, got, slot)
        groups.append(jnp.where(slot >= OWNED, -1, slot))
    near = own_ref[1, pl.ds(16, 4), :].astype(jnp.int32)
    near = jnp.where(near < OWNED, near, -1)
    core = jnp.concatenate(
        [center_ref[:, r * LANES : (r + 1) * LANES] for r in range(4)], axis=0
    )
    groups.append(jnp.concatenate([near, core], axis=0))
    for q in range(5):
        slot = groups[q]
        slot_ref[pl.ds(8 * q, 8), :] = slot
        late = slot - SLOTS
        is_late = late >= 0
        high = jnp.where(is_late, KEPT_ROWS + (late >> 6), slot >> 7)
        low_a = jnp.where(is_late, late & 63, slot & 127)
        low_b = jnp.where(is_late, (late & 63) + MOVES, slot & 127)
        found = [jnp.zeros((8, LANES), F32) for _ in range(4)]
        for h in range(KEPT_ROWS + 8):
            here = high == h
            for c in range(4):
                if h < KEPT_ROWS:
                    row = kept_ref[c, pl.ds(h, 1), :]
                else:
                    row = arrive_ref[c // 2, pl.ds(h - KEPT_ROWS, 1), :]
                got = lane_pick(row, low_b if c % 2 else low_a)
                found[c] = jnp.where(here, got, found[c])
        for half in range(2):
            item = 2 * q + half
            for c in range(4):
                rows = found[c][4 * half : 4 * half + 4, :]
                if item < 8:
                    dx, dy = DIRS[item]
                    ref = {-1: left_ref, 0: same_ref, 1: right_ref}[dx]
                    ref[dy + 1, pl.ds(4 * c, 4), :] = rows
                elif item == 8:
                    same_ref[1, pl.ds(4 * c, 4), :] = rows
                else:
                    center_out[pl.ds(4 * c, 4), :] = rows


def edge_kernel(
    layers,
    blocks_ref, same_ref, below_ref, above_ref, center_ref, core_row_ref, core_col_ref,
    w_in_t_ref, w_rad_ref, w_two_t_ref, w_two_ref, w_mix_t_ref, w_mix_ref, w_up_t_ref,
    w_up_ref, w_out_ref,
    msg_ref,
    lhs_ref, rhs_ref, back_ref, joined_ref, latent_ref, d_latent_ref, edge_mix_ref, env_mix_ref,
    pooled_ref, act_ref, slope_ref,
):
    near = same_ref[1] + below_ref[...] + above_ref[...]
    mid = center_ref[...]

    def flat(rows, c):
        return jnp.concatenate([rows[4 * c + r : 4 * c + r + 1, :] for r in range(4)], axis=1)

    delta = [flat(near, c) - flat(mid, c) for c in range(3)]
    kind_n, kind_c = flat(near, 3), flat(mid, 3)
    radius = jnp.sqrt(delta[0] * delta[0] + delta[1] * delta[1] + delta[2] * delta[2] + SOFTENING)
    inv_radius = 1.0 / radius
    block = lax.broadcasted_iota(jnp.int32, (1, EDGES), 1) >> 7
    live = (block < blocks_ref[0]) & (kind_c > 0.5) & (kind_n > 0.5)
    live = jnp.where(live, 1.0, 0.0)
    ramp = jnp.maximum(0.0, 1.0 - radius * radius / (CUTOFF * CUTOFF))
    envelope = live * ramp * ramp
    ux, uy, uz = (d * (1.0 / CUTOFF) for d in delta)
    sph = [
        ROOT3 * ux,
        ROOT3 * uy,
        ROOT3 * uz,
        ROOT15 * ux * uy,
        ROOT15 * uy * uz,
        ROOT15 * ux * uz,
        (0.5 * ROOT5) * (2.0 * uz * uz - ux * ux - uy * uy),
        (0.5 * ROOT15) * (ux * ux - uy * uy),
    ]
    q8 = lax.broadcasted_iota(jnp.int32, (8, EDGES), 0)
    shift = radius - q8.astype(F32) * (CUTOFF / 7.0)
    radial = jnp.exp(-(shift * shift) * (1.0 / (BASIS_WIDTH * BASIS_WIDTH)))
    ids = (q8 & 3) + 1
    kinds = jnp.where(q8 < 4, kind_c, kind_n)
    onehot = jnp.where(kinds == ids.astype(F32), 1.0, 0.0)
    same_center = core_col_ref[...] == core_row_ref[...]
    zero_row = jnp.zeros((1, EDGES), F32)

    def gram(rows):
        top, rest = [], []
        for row in rows:
            a, b = split(row)
            top.append(a.astype(F32))
            rest.append(b.astype(F32))
        fill = [jnp.zeros((LANES - 3 * len(rows), EDGES), F32)]
        a = jnp.concatenate(top + top + rest + fill, axis=0).astype(BF16)
        b = jnp.concatenate(top + rest + top + fill, axis=0).astype(BF16)
        return jnp.where(same_center, mm(a, b, TN), 0.0).astype(BF16)

    grams = [jnp.where(same_center, 1.0, 0.0).astype(BF16), gram(sph[:3]), gram(sph[3:])]

    feats = jnp.concatenate([radial, onehot, jnp.zeros((LANES - 16, EDGES), F32)], axis=0)
    pre = mm_high(w_in_t_ref[...], feats)

    def sigmoid(x):
        return 0.5 * jnp.tanh(0.5 * x) + 0.5

    gate0 = sigmoid(pre)
    hidden = (pre * gate0).astype(BF16)
    slope0 = gate0 * (1.0 + pre * (1.0 - gate0))
    two = mm(w_two_t_ref[...], hidden)
    gate1 = sigmoid(two)
    act1 = two * gate1
    slope1 = gate1 * (1.0 + two * (1.0 - gate1))
    latent_ref[...] = act1 * envelope
    spare = jnp.zeros((64, EDGES), BF16)

    def forward(t, carry):
        latent = latent_ref[...]
        latent_b = latent.astype(BF16)
        mixed = mm(w_mix_t_ref[t], latent_b)
        edge_mix, env_mix = mixed[:192, :], mixed[192:, :].astype(BF16)
        pooled = jnp.concatenate(
            [mm(env_mix[64 * l : 64 * l + 64, :], grams[l]) for l in range(3)], axis=0
        ) * ENV_SCALE
        invariants = (edge_mix * pooled).astype(BF16)
        update = mm(w_up_t_ref[t], jnp.concatenate([latent_b, invariants, spare], axis=0))
        gate = sigmoid(update)
        act = update * gate
        edge_mix_ref[t] = edge_mix
        env_mix_ref[t] = env_mix
        pooled_ref[t] = pooled
        act_ref[t] = act
        slope_ref[t] = gate * (1.0 + update * (1.0 - gate))
        latent_ref[...] = latent + act * envelope
        return carry

    lax.fori_loop(0, layers, forward, 0)
    w_out = w_out_ref[...]
    read = jnp.sum(latent_ref[...].astype(BF16).astype(F32) * w_out, axis=0, keepdims=True)
    energy = envelope * read
    d_latent_ref[...] = (w_out * envelope).astype(BF16).astype(F32)

    def backward(s, d_env):
        t = layers - 1 - s
        d_latent = d_latent_ref[...]
        d_env = d_env + jnp.sum(d_latent * act_ref[t], axis=0, keepdims=True)
        d_update = (d_latent * envelope * slope_ref[t]).astype(BF16)
        joined_ref[...] = mm(w_up_ref[t], d_update)
        d_inv = joined_ref[pl.ds(256, 192), :]
        d_edge_mix = (d_inv * pooled_ref[t]).astype(BF16)
        d_pooled = (d_inv * edge_mix_ref[t] * ENV_SCALE).astype(BF16)
        d_env_mix = jnp.concatenate(
            [mm(d_pooled[64 * l : 64 * l + 64, :], grams[l]) for l in range(3)], axis=0
        ).astype(BF16)
        for l in range(1, 3):
            mix_l = env_mix_ref[t, pl.ds(64 * l, 64), :]
            pool_l = d_pooled[64 * l : 64 * l + 64, :]
            lhs_ref[l - 1, t] = jnp.concatenate([pool_l, mix_l], axis=0)
            rhs_ref[l - 1, t] = jnp.concatenate([mix_l, pool_l], axis=0)
        back_ref[...] = mm(
            w_mix_ref[t], jnp.concatenate([d_edge_mix, d_env_mix, spare, spare], axis=0)
        )
        d_latent_ref[...] = d_latent + joined_ref[pl.ds(0, 256), :] + back_ref[...]
        return d_env

    d_env = lax.fori_loop(0, layers, backward, read)
    d_latent = d_latent_ref[...]
    d_env = d_env + jnp.sum(d_latent * act1, axis=0, keepdims=True)
    d_two = (d_latent * envelope * slope1).astype(BF16)
    d_pre = mm(w_two_ref[...], d_two) * slope0
    d_radial = mm_high(w_rad_ref[...], d_pre)
    d_radius = jnp.sum(
        d_radial * radial * shift, axis=0, keepdims=True
    ) * (-2.0 / (BASIS_WIDTH * BASIS_WIDTH))
    d_radius = d_radius - d_env * live * ramp * radius * (4.0 / (CUTOFF * CUTOFF))

    def both(ref, l):
        return jnp.concatenate([ref[l - 1, t] for t in range(layers)], axis=0)

    d_sph = []
    for l, rows in ((1, sph[:3]), (2, sph[3:])):
        pairs = jnp.where(same_center, mm(both(lhs_ref, l), both(rhs_ref, l), TN), 0.0)
        top, rest = split(pairs)
        fill = [zero_row] * (8 - len(rows))
        ya, yb = split(jnp.concatenate(list(rows) + fill, axis=0))
        got = mm(ya, top) + mm(yb, top) + mm(ya, rest)
        d_sph += [got[i : i + 1, :] for i in range(len(rows))]
    d1, d2, d3, d4, d5, d6, d7, d8 = d_sph
    du = [
        ROOT3 * d1 + ROOT15 * (uy * d4 + uz * d6 + ux * d8) - ROOT5 * ux * d7,
        ROOT3 * d2 + ROOT15 * (ux * d4 + uz * d5 - uy * d8) - ROOT5 * uy * d7,
        ROOT3 * d3 + ROOT15 * (uy * d5 + ux * d6) + (2.0 * ROOT5) * uz * d7,
    ]
    scale = d_radius * inv_radius
    for c in range(3):
        grad = scale * delta[c] + du[c] * (1.0 / CUTOFF)
        for r in range(4):
            msg_ref[pl.ds(4 * c + r, 1), :] = grad[:, r * LANES : (r + 1) * LANES]
    for r in range(4):
        msg_ref[pl.ds(12 + r, 1), :] = energy[:, r * LANES : (r + 1) * LANES]


def spread(slot_rows, value_rows):
    chans = len(value_rows[0])
    sub32 = lax.broadcasted_iota(jnp.int32, (32, LANES), 0)
    sub128 = lax.broadcasted_iota(jnp.int32, (LANES, LANES), 0)
    total = jnp.zeros((2 * chans * 32, LANES), F32)
    for first in range(0, len(slot_rows), 2):
        a_parts, b_parts = [], []
        for slot, values in zip(slot_rows[first : first + 2], value_rows[first : first + 2]):
            here = sub32 == (slot >> 7)
            pieces = []
            for value in values:
                top, rest = split(value)
                pieces.append(jnp.where(here, top.astype(F32), 0.0))
                pieces.append(jnp.where(here, rest.astype(F32), 0.0))
            a_parts.append(jnp.concatenate(pieces, axis=0))
            b_parts.append(jnp.where(sub128 == (slot & 127), 1.0, 0.0))
        a = jnp.concatenate(a_parts, axis=1).astype(BF16)
        b = jnp.concatenate(b_parts, axis=1).astype(BF16)
        total = total + mm(a, b, NT)
    return [total[64 * c : 64 * c + 32, :] + total[64 * c + 32 : 64 * c + 64, :] for c in range(chans)]


def store_flat(ref, lead, table):
    for h in range(27):
        stop = min((h + 1) * LANES, OWNED)
        ref[lead + (slice(None), slice(h * LANES, stop))] = table[h : h + 1, : stop - h * LANES]


def home_kernel(msg_ref, slot_ref, force_ref, atom_ref):
    slot_rows, value_rows, energies = [], [], []
    for r in range(4):
        grads = [msg_ref[pl.ds(4 * c + r, 1), :] for c in range(3)]
        slot_rows.append(slot_ref[pl.ds(32 + r, 1), :])
        value_rows.append([-g for g in grads])
    for r in range(4):
        grads = [msg_ref[pl.ds(4 * c + r, 1), :] for c in range(3)]
        slot_rows.append(slot_ref[pl.ds(36 + r, 1), :])
        value_rows.append(grads)
    for c, table in enumerate(spread(slot_rows, value_rows)):
        force_ref[c] = table
    energies = [[msg_ref[pl.ds(12 + r, 1), :]] for r in range(4)]
    store_flat(atom_ref, (0,), spread(slot_rows[4:], energies)[0])


def return_kernel(own_ref, below_ref, above_ref, slot_ref, force_in_ref, force_ref):
    by_dy = {-1: below_ref, 0: own_ref, 1: above_ref}
    slot_rows, value_rows = [], []
    for o, (dx, dy) in enumerate(DIRS):
        for r in range(4):
            slot_rows.append(slot_ref[pl.ds(4 * o + r, 1), :])
            value_rows.append(
                [by_dy[dy][dx + 1, pl.ds(4 * c + r, 1), :] for c in range(3)]
            )
    for c, table in enumerate(spread(slot_rows, value_rows)):
        store_flat(force_ref, (c,), force_in_ref[c] - table)


def whole(count, smem=()):
    return [
        pl.BlockSpec(memory_space=pltpu.SMEM if i in smem else pltpu.VMEM) for i in range(count)
    ]


def call(kernel, outs, args, smem=(), scratch=(), cost=None):
    many = isinstance(outs, (list, tuple))
    return pl.pallas_call(
        kernel,
        out_shape=outs,
        in_specs=whole(len(args), smem),
        out_specs=whole(len(outs)) if many else whole(1)[0],
        scratch_shapes=list(scratch),
        compiler_params=pltpu.CompilerParams(vmem_limit_bytes=VMEM_LIMIT),
    )(*args)


def shift(x, axis, step):
    count = lax.axis_size(axis)
    return lax.ppermute(x, axis, [(i, (i + step) % count) for i in range(count)])


def around(x, axis):
    return shift(x, axis, 1), shift(x, axis, -1)


def shaped(*dims, dtype=F32):
    return jax.ShapeDtypeStruct(dims, dtype)


def per_device(
    positions,
    species,
    mig_rows,
    ghost_rows,
    edge_center,
    edge_neighbor,
    edge_blocks,
    w_radial,
    w_kind_center,
    w_kind_neigh,
    w_two,
    w_edge,
    w_env,
    w_update,
    w_out,
):
    layers = w_edge.shape[0]
    pos = positions.reshape(3, 1, SLOTS)
    kind = species.reshape(1, SLOTS)
    mig = mig_rows.reshape(8, MOVES)
    ghosts = ghost_rows.reshape(8, GHOSTS)
    centers = edge_center.reshape(1, EDGES)
    nbrs = edge_neighbor.reshape(1, EDGES)
    blocks = edge_blocks.reshape(1)
    grid = (lax.axis_size("gx"), lax.axis_size("gy"))
    place = jnp.stack([lax.axis_index("gx"), lax.axis_index("gy")]).astype(jnp.int32)

    msg = call(send_kernel, shaped(24, LANES), (pos, kind, mig, nbrs))
    left, right = around(msg, "gx")
    column = jnp.stack([left, msg, right])
    kept = call(keep_kernel, shaped(4, 24, LANES), (pos, kind, mig))
    below, above = around(column, "gy")

    to_left, to_right, same, mids, slots, arrived = call(
        lambda *refs: answer_kernel(grid, *refs),
        (
            shaped(3, 16, LANES),
            shaped(3, 16, LANES),
            shaped(3, 16, LANES),
            shaped(16, LANES),
            shaped(40, LANES, dtype=jnp.int32),
            shaped(2, 8, LANES),
        ),
        (place, column, below, above, ghosts, centers, kept),
        smem=(0,),
    )
    from_left = shift(to_right, "gx", 1)
    from_right = shift(to_left, "gx", -1)
    same = same + from_left + from_right
    from_below = shift(same[2], "gy", 1)
    from_above = shift(same[0], "gy", -1)

    stay = kept[:3].reshape(3, 24 * LANES)[:, :SLOTS]
    late = arrived.reshape(2, 8, 2, MOVES).transpose(0, 2, 1, 3).reshape(4, 8 * MOVES)[:3]
    owned_positions = jnp.concatenate([stay, late], 1).reshape(3, 1, 1, OWNED)

    w_in = jnp.concatenate([w_radial, w_kind_center, w_kind_neigh], 0)
    w_in_t = jnp.pad(w_in, ((0, LANES - 16), (0, 0))).T
    w_mix = jnp.concatenate([w_edge, w_env], 2)
    w_mix_wide = jnp.pad(w_mix, ((0, 0), (0, 0), (0, LANES)))
    w_up_t = jnp.pad(w_update, ((0, 0), (0, 64), (0, 0))).transpose(0, 2, 1)
    grad = call(
        lambda *refs: edge_kernel(layers, *refs),
        shaped(16, LANES),
        (
            blocks, same, from_below, from_above, mids, centers, edge_center.reshape(EDGES, 1),
            w_in_t, w_radial, w_two.T, w_two, w_mix.transpose(0, 2, 1), w_mix_wide, w_up_t, w_update,
            w_out.astype(F32).reshape(-1, 1),
        ),
        smem=(0,),
        scratch=(
            pltpu.VMEM((2, layers, 128, EDGES), BF16),
            pltpu.VMEM((2, layers, 128, EDGES), BF16),
            pltpu.VMEM((256, EDGES), F32),
            pltpu.VMEM((448, EDGES), F32),
            pltpu.VMEM((256, EDGES), F32),
            pltpu.VMEM((256, EDGES), F32),
            pltpu.VMEM((layers, 192, EDGES), F32),
            pltpu.VMEM((layers, 192, EDGES), BF16),
            pltpu.VMEM((layers, 192, EDGES), F32),
            pltpu.VMEM((layers, 256, EDGES), F32),
            pltpu.VMEM((layers, 256, EDGES), F32),
        ),
    )
    left, right = around(grad, "gx")
    column = jnp.stack([left, grad, right])
    force_home, atoms = call(
        home_kernel, (shaped(3, 32, LANES), shaped(1, 1, OWNED)), (grad, slots)
    )
    below, above = around(column, "gy")
    forces = call(
        return_kernel, shaped(3, 1, OWNED), (column, below, above, slots, force_home)
    )
    return (owned_positions, forces.reshape(3, 1, 1, OWNED), atoms)


def solution(mesh):
    placed = (
        P(None, "gx", "gy", None),
        P("gx", "gy", None),
        P("gx", "gy", None, None),
        P("gx", "gy", None, None),
        P("gx", "gy", None),
        P("gx", "gy", None),
        P("gx", "gy"),
        P(),
        P(),
        P(),
        P(),
        P(),
        P(),
        P(),
        P(),
    )
    return jax.shard_map(
        per_device,
        mesh=mesh,
        in_specs=placed,
        out_specs=(P(None, "gx", "gy", None), P(None, "gx", "gy", None), P("gx", "gy", None)),
        check_vma=False,
    )
```

```python
import math

import jax
import jax.numpy as jnp
from jax import lax
from jax.experimental import pallas as pl
from jax.experimental.pallas import tpu as pltpu
from jax.sharding import PartitionSpec as P

CUTOFF = 6.0
SOFTENING = 0.01
BASIS_WIDTH = 0.8
ENV_SCALE = 0.3
ROOT3 = math.sqrt(3.0)
ROOT5 = math.sqrt(5.0)
ROOT15 = math.sqrt(15.0)
DIRS = ((-1, -1), (-1, 0), (-1, 1), (0, -1), (0, 1), (1, -1), (1, 0), (1, 1))
SLOTS = 2940
MOVES = 64
OWNED = 3452
GHOSTS = 1260
EDGES = 512
LANES = 128
KEPT_ROWS = 23
F32 = jnp.float32
BF16 = jnp.bfloat16
VMEM_LIMIT = 48 * 1024 * 1024
WHOLE_VMEM = 64 * 1024 * 1024

NN = (((1,), (0,)), ((), ()))
NT = (((1,), (1,)), ((), ()))
TN = (((0,), (0,)), ((), ()))


def mm(a, b, dims=NN):
    return lax.dot_general(a, b, dims, preferred_element_type=F32)


def split(x):
    top = x.astype(BF16)
    return top, (x - top.astype(F32)).astype(BF16)


def halves(x):
    top = x.astype(BF16).astype(F32)
    return top, x - top


def lane_pick(row, low):
    table = jnp.broadcast_to(row, low.shape)
    return jnp.take_along_axis(table, low, axis=1, mode="promise_in_bounds")


def full_row(ref, lead, start, size):
    stop = min(start + LANES, size)
    piece = ref[lead + (slice(None), slice(start, stop))]
    if stop - start < LANES:
        pad = jnp.zeros((1, LANES - (stop - start)), piece.dtype)
        piece = jnp.concatenate([piece, pad], axis=1)
    return piece


def payload_row(pos_ref, kind_ref, chan, h):
    if chan < 3:
        return full_row(pos_ref, (chan,), h * LANES, SLOTS)
    return full_row(kind_ref, (), h * LANES, SLOTS).astype(F32)


def send_kernel(pos_hbm, kind_hbm, mig_hbm, nbr_hbm, msg_ref, pos_ref, kind_ref, mig_ref, nbr_ref, sems):
    copies = [
        pltpu.make_async_copy(a, b, sems.at[i])
        for i, (a, b) in enumerate(
            ((mig_hbm, mig_ref), (nbr_hbm, nbr_ref), (kind_hbm, kind_ref), (pos_hbm, pos_ref))
        )
    ]
    for copy in copies:
        copy.start()
    copies[0].wait()
    rows = mig_ref[...]
    rows = jnp.concatenate([rows, jnp.full((8, LANES - MOVES), -1, jnp.int32)], axis=1)
    high, low = rows >> 7, rows & 127
    copies[1].wait()
    for r in range(4):
        msg_ref[pl.ds(16 + r, 1), :] = nbr_ref[:, r * LANES : (r + 1) * LANES].astype(F32)
    msg_ref[pl.ds(20, 4), :] = jnp.zeros((4, LANES), F32)
    copies[2].wait()
    copies[3].wait()
    picked = [jnp.zeros((8, LANES), F32) for _ in range(4)]
    for h in range(KEPT_ROWS):
        here = high == h
        for c in range(4):
            got = lane_pick(payload_row(pos_ref, kind_ref, c, h), low)
            picked[c] = jnp.where(here, got, picked[c])
    for p in range(2):
        msg_ref[pl.ds(8 * p, 8), :] = picked[2 * p] + pltpu.roll(picked[2 * p + 1], MOVES, 1)


def keep_kernel(pos_ref, kind_ref, mig_ref, kept_ref):
    rows = mig_ref[...]
    rows = jnp.concatenate([rows, jnp.full((8, LANES - MOVES), -1, jnp.int32)], axis=1)
    high, low = rows >> 7, rows & 127
    sub32 = lax.broadcasted_iota(jnp.int32, (32, LANES), 0)
    sub128 = lax.broadcasted_iota(jnp.int32, (LANES, LANES), 0)
    left = jnp.zeros((32, LANES), F32)
    for k in range(8):
        a = (sub32 == high[k : k + 1, :]).astype(F32).astype(BF16)
        b = (sub128 == low[k : k + 1, :]).astype(F32).astype(BF16)
        left = left + mm(a, b, NT)
    stay = left < 0.5
    for c in range(4):
        table = jnp.concatenate(
            [payload_row(pos_ref, kind_ref, c, h) for h in range(KEPT_ROWS)]
            + [jnp.zeros((1, LANES), F32)],
            axis=0,
        )
        kept_ref[c] = jnp.where(stay[:24, :], table, 0.0)


def arrange(ix, iy, own_ref, even_ref, odd_ref, grid_ref):
    odd_x, odd_y = ix & 1, iy & 1
    for dx in (-1, 0, 1):
        block = {-1: 2 - 2 * odd_x, 0: 1, 1: 2 * odd_x}[dx]
        even, odd = even_ref[block], odd_ref[block]
        grid_ref[0, dx + 1] = jnp.where(odd_y > 0, even, odd)
        grid_ref[1, dx + 1] = own_ref[block]
        grid_ref[2, dx + 1] = jnp.where(odd_y > 0, odd, even)


def answer_kernel(
    grid, where_ref, own_ref, even_ref, odd_ref, ghost_ref, center_ref, kept_ref,
    to_even_ref, to_odd_ref, same_ref, center_out, slot_ref, arrive_ref, grid_ref,
):
    nx, ny = grid
    ix, iy = where_ref[0], where_ref[1]
    arrange(ix, iy, own_ref, even_ref, odd_ref, grid_ref)
    inside = []
    for dx, dy in DIRS:
        ok = (ix + dx >= 0) & (ix + dx < nx) & (iy + dy >= 0) & (iy + dy < ny)
        inside.append(ok.astype(jnp.int32))
    for p in range(2):
        for k, (dx, dy) in enumerate(DIRS):
            row = grid_ref[dy + 1, dx + 1, pl.ds(8 * p + 7 - k, 1), :]
            arrive_ref[p, pl.ds(k, 1), :] = row * inside[k].astype(F32)
    groups = []
    for o in range(0, 8, 2):
        parts = []
        for d in (o, o + 1):
            dx, dy = DIRS[d]
            listed = grid_ref[dy + 1, dx + 1, pl.ds(16, 4), :].astype(jnp.int32)
            rank = listed - (OWNED + GHOSTS * (7 - d))
            ok = (rank >= 0) & (rank < GHOSTS) & (inside[d] > 0)
            parts.append(jnp.where(ok, rank, -1))
        rank = jnp.concatenate(parts, axis=0)
        high, low = rank >> 7, rank & 127
        slot = jnp.full((8, LANES), -1, jnp.int32)
        upper = lax.broadcasted_iota(jnp.int32, (8, LANES), 0) < 4
        for h in range(10):
            stop = min((h + 1) * LANES, GHOSTS)
            pair = []
            for d in (o, o + 1):
                row = ghost_ref[pl.ds(d, 1), h * LANES : stop]
                if stop - h * LANES < LANES:
                    pad = jnp.full((1, LANES - (stop - h * LANES)), -1, jnp.int32)
                    row = jnp.concatenate([row, pad], axis=1)
                pair.append(jnp.broadcast_to(row, (8, LANES)))
            table = jnp.where(upper, pair[0], pair[1])
            got = jnp.take_along_axis(table, low, axis=1, mode="promise_in_bounds")
            slot = jnp.where(high == h, got, slot)
        groups.append(jnp.where(slot >= OWNED, -1, slot))
    near = own_ref[1, pl.ds(16, 4), :].astype(jnp.int32)
    near = jnp.where(near < OWNED, near, -1)
    core = jnp.concatenate(
        [center_ref[:, r * LANES : (r + 1) * LANES] for r in range(4)], axis=0
    )
    groups.append(jnp.concatenate([near, core], axis=0))
    sides = {-1: [], 0: [], 1: []}
    for q in range(5):
        slot = groups[q]
        slot_ref[pl.ds(8 * q, 8), :] = slot
        late = slot - SLOTS
        is_late = late >= 0
        high = jnp.where(is_late, KEPT_ROWS + (late >> 6), slot >> 7)
        low_a = jnp.where(is_late, late & 63, slot & 127)
        low_b = jnp.where(is_late, (late & 63) + MOVES, slot & 127)
        found = [jnp.zeros((8, LANES), F32) for _ in range(4)]
        for h in range(KEPT_ROWS + 8):
            here = high == h
            for c in range(4):
                if h < KEPT_ROWS:
                    row = kept_ref[c, pl.ds(h, 1), :]
                else:
                    row = arrive_ref[c // 2, pl.ds(h - KEPT_ROWS, 1), :]
                got = lane_pick(row, low_b if c % 2 else low_a)
                found[c] = jnp.where(here, got, found[c])
        for half in range(2):
            item = 2 * q + half
            for c in range(4):
                rows = found[c][4 * half : 4 * half + 4, :]
                if item < 8:
                    dx, dy = DIRS[item]
                    if dx == 0:
                        same_ref[dy + 1, pl.ds(4 * c, 4), :] = rows
                    sides[dx].append((dy + 1, 4 * c, rows))
                elif item == 8:
                    same_ref[1, pl.ds(4 * c, 4), :] = rows
                else:
                    center_out[pl.ds(4 * c, 4), :] = rows
    flip = (ix & 1) > 0
    for (d, start, left), (_, _, right) in zip(sides[-1], sides[1]):
        to_even_ref[d, pl.ds(start, 4), :] = jnp.where(flip, left, right)
        to_odd_ref[d, pl.ds(start, 4), :] = jnp.where(flip, right, left)


def edge_kernel(
    layers,
    blocks_ref, same_ref, below_ref, above_ref, center_ref, core_row_ref, core_col_ref,
    w_rad_ref, w_kc_ref, w_kn_ref, w_two_ref, w_edge_t_ref, w_env_t_ref, w_up_ref, w_out_ref,
    msg_ref,
    lhs_ref, rhs_ref, back_ref, joined_ref, latent_ref, d_latent_ref, edge_mix_ref, env_mix_ref,
    pooled_ref, act_ref, slope_ref,
):
    near = same_ref[1] + below_ref[...] + above_ref[...]
    mid = center_ref[...]

    def flat(rows, c):
        return jnp.concatenate([rows[4 * c + r : 4 * c + r + 1, :] for r in range(4)], axis=1)

    delta = [flat(near, c) - flat(mid, c) for c in range(3)]
    kind_n, kind_c = flat(near, 3), flat(mid, 3)
    radius = jnp.sqrt(delta[0] * delta[0] + delta[1] * delta[1] + delta[2] * delta[2] + SOFTENING)
    inv_radius = 1.0 / radius
    block = lax.broadcasted_iota(jnp.int32, (1, EDGES), 1) >> 7
    live = (block < blocks_ref[0]) & (kind_c > 0.5) & (kind_n > 0.5)
    live = jnp.where(live, 1.0, 0.0)
    ramp = jnp.maximum(0.0, 1.0 - radius * radius / (CUTOFF * CUTOFF))
    envelope = live * ramp * ramp
    ux, uy, uz = (d * (1.0 / CUTOFF) for d in delta)
    sph = [
        ROOT3 * ux,
        ROOT3 * uy,
        ROOT3 * uz,
        ROOT15 * ux * uy,
        ROOT15 * uy * uz,
        ROOT15 * ux * uz,
        (0.5 * ROOT5) * (2.0 * uz * uz - ux * ux - uy * uy),
        (0.5 * ROOT15) * (ux * ux - uy * uy),
    ]
    q8 = lax.broadcasted_iota(jnp.int32, (8, EDGES), 0)
    shift = radius - q8.astype(F32) * (CUTOFF / 7.0)
    radial = jnp.exp(-(shift * shift) * (1.0 / (BASIS_WIDTH * BASIS_WIDTH)))
    ids = (q8 & 3) + 1
    kinds = jnp.where(q8 < 4, kind_c, kind_n)
    onehot = jnp.where(kinds == ids.astype(F32), 1.0, 0.0)
    same_center = core_col_ref[...] == core_row_ref[...]
    zero_row = jnp.zeros((1, EDGES), F32)

    def gram(rows):
        top, rest = [], []
        for row in rows:
            a, b = split(row)
            top.append(a.astype(F32))
            rest.append(b.astype(F32))
        fill = [jnp.zeros((LANES - 3 * len(rows), EDGES), F32)]
        a = jnp.concatenate(top + top + rest + fill, axis=0).astype(BF16)
        b = jnp.concatenate(top + rest + top + fill, axis=0).astype(BF16)
        return jnp.where(same_center, mm(a, b, TN), 0.0).astype(BF16)

    grams = [jnp.where(same_center, 1.0, 0.0).astype(BF16), gram(sph[:3]), gram(sph[3:])]

    w_top, w_rest = halves(
        jnp.concatenate([w_rad_ref[...], w_kc_ref[...], w_kn_ref[...]], axis=0)
    )
    f_top, f_rest = halves(jnp.concatenate([radial, onehot], axis=0))
    w_in = jnp.concatenate([w_top, w_rest, w_top, jnp.zeros((LANES - 48, 256), F32)], axis=0)
    feats = jnp.concatenate([f_top, f_top, f_rest, jnp.zeros((LANES - 48, EDGES), F32)], axis=0)
    pre = mm(w_in.astype(BF16), feats.astype(BF16), TN)

    def sigmoid(x):
        return 0.5 * jnp.tanh(0.5 * x) + 0.5

    gate0 = sigmoid(pre)
    hidden = (pre * gate0).astype(BF16)
    slope0 = gate0 * (1.0 + pre * (1.0 - gate0))
    two = mm(w_two_ref[...], hidden, TN)
    gate1 = sigmoid(two)
    act1 = two * gate1
    slope1 = gate1 * (1.0 + two * (1.0 - gate1))
    latent_ref[...] = act1 * envelope

    def forward(t, carry):
        latent = latent_ref[...]
        latent_b = latent.astype(BF16)
        edge_mix = mm(w_edge_t_ref[t], latent_b)
        env_mix = mm(w_env_t_ref[t], latent_b).astype(BF16)
        pooled = jnp.concatenate(
            [mm(env_mix[64 * l : 64 * l + 64, :], grams[l]) for l in range(3)], axis=0
        ) * ENV_SCALE
        invariants = (edge_mix * pooled).astype(BF16)
        update = mm(w_up_ref[t], jnp.concatenate([latent_b, invariants], axis=0), TN)
        gate = sigmoid(update)
        act = update * gate
        edge_mix_ref[t] = edge_mix
        env_mix_ref[t] = env_mix
        pooled_ref[t] = pooled
        act_ref[t] = act
        slope_ref[t] = gate * (1.0 + update * (1.0 - gate))
        latent_ref[...] = latent + act * envelope
        return carry

    lax.fori_loop(0, layers, forward, 0)
    w_out = w_out_ref[...]
    read = jnp.sum(latent_ref[...].astype(BF16).astype(F32) * w_out, axis=0, keepdims=True)
    energy = envelope * read
    d_latent_ref[...] = (w_out * envelope).astype(BF16).astype(F32)

    def backward(s, d_env):
        t = layers - 1 - s
        d_latent = d_latent_ref[...]
        d_env = d_env + jnp.sum(d_latent * act_ref[t], axis=0, keepdims=True)
        d_update = (d_latent * envelope * slope_ref[t]).astype(BF16)
        joined_ref[...] = mm(w_up_ref[t], d_update)
        d_inv = joined_ref[pl.ds(256, 192), :]
        d_edge_mix = (d_inv * pooled_ref[t]).astype(BF16)
        d_pooled = (d_inv * edge_mix_ref[t] * ENV_SCALE).astype(BF16)
        d_env_mix = jnp.concatenate(
            [mm(d_pooled[64 * l : 64 * l + 64, :], grams[l]) for l in range(3)], axis=0
        ).astype(BF16)
        for l in range(1, 3):
            mix_l = env_mix_ref[t, pl.ds(64 * l, 64), :]
            pool_l = d_pooled[64 * l : 64 * l + 64, :]
            lhs_ref[l - 1, t] = jnp.concatenate([pool_l, mix_l], axis=0)
            rhs_ref[l - 1, t] = jnp.concatenate([mix_l, pool_l], axis=0)
        back_ref[...] = mm(
            jnp.concatenate([w_edge_t_ref[t], w_env_t_ref[t]], axis=0),
            jnp.concatenate([d_edge_mix, d_env_mix], axis=0),
            TN,
        )
        d_latent_ref[...] = d_latent + joined_ref[pl.ds(0, 256), :] + back_ref[...]
        return d_env

    d_env = lax.fori_loop(0, layers, backward, read)
    d_latent = d_latent_ref[...]
    d_env = d_env + jnp.sum(d_latent * act1, axis=0, keepdims=True)
    d_two = (d_latent * envelope * slope1).astype(BF16)
    d_pre = mm(w_two_ref[...], d_two) * slope0
    w_back = jnp.concatenate([w_top[:8, :], w_rest[:8, :]], axis=0).astype(BF16)
    d_radial = mm(w_back, d_pre.astype(BF16))
    d_radial = d_radial[:8, :] + d_radial[8:, :]
    d_radius = jnp.sum(
        d_radial * radial * shift, axis=0, keepdims=True
    ) * (-2.0 / (BASIS_WIDTH * BASIS_WIDTH))
    d_radius = d_radius - d_env * live * ramp * radius * (4.0 / (CUTOFF * CUTOFF))

    def both(ref, l):
        return jnp.concatenate([ref[l - 1, t] for t in range(layers)], axis=0)

    d_sph = []
    for l, rows in ((1, sph[:3]), (2, sph[3:])):
        pairs = jnp.where(same_center, mm(both(lhs_ref, l), both(rhs_ref, l), TN), 0.0)
        fill = [zero_row] * (8 - len(rows))
        y_top, y_rest = halves(jnp.concatenate(list(rows) + fill, axis=0))
        got = mm(jnp.concatenate([y_top, y_rest], axis=0).astype(BF16), pairs.astype(BF16))
        got = got[:8, :] + got[8:, :]
        d_sph += [got[i : i + 1, :] for i in range(len(rows))]
    d1, d2, d3, d4, d5, d6, d7, d8 = d_sph
    du = [
        ROOT3 * d1 + ROOT15 * (uy * d4 + uz * d6 + ux * d8) - ROOT5 * ux * d7,
        ROOT3 * d2 + ROOT15 * (ux * d4 + uz * d5 - uy * d8) - ROOT5 * uy * d7,
        ROOT3 * d3 + ROOT15 * (uy * d5 + ux * d6) + (2.0 * ROOT5) * uz * d7,
    ]
    scale = d_radius * inv_radius
    for c in range(3):
        grad = scale * delta[c] + du[c] * (1.0 / CUTOFF)
        for r in range(4):
            msg_ref[pl.ds(4 * c + r, 1), :] = grad[:, r * LANES : (r + 1) * LANES]
    for r in range(4):
        msg_ref[pl.ds(12 + r, 1), :] = energy[:, r * LANES : (r + 1) * LANES]


def spread(entries, chans):
    sub32 = lax.broadcasted_iota(jnp.int32, (32, LANES), 0)
    sub128 = lax.broadcasted_iota(jnp.int32, (LANES, LANES), 0)
    pieces = len(entries[0][2]) // chans
    total = jnp.zeros((pieces * chans * 32, LANES), F32)
    for first in range(0, len(entries), 2):
        a_parts, b_parts = [], []
        for high, low, values in entries[first : first + 2]:
            here = sub32 == high
            a_parts.append(jnp.concatenate([jnp.where(here, v, 0.0) for v in values], axis=0))
            b_parts.append(jnp.where(sub128 == low, 1.0, 0.0))
        a = jnp.concatenate(a_parts, axis=1).astype(BF16)
        b = jnp.concatenate(b_parts, axis=1).astype(BF16)
        total = total + mm(a, b, NT)
    tables = [total[32 * i : 32 * i + 32, :] for i in range(pieces * chans)]
    return [sum(tables[c * pieces + 1 : (c + 1) * pieces], tables[c * pieces]) for c in range(chans)]


def store_flat(ref, lead, table):
    for h in range(27):
        stop = min((h + 1) * LANES, OWNED)
        ref[lead + (slice(None), slice(h * LANES, stop))] = table[h : h + 1, : stop - h * LANES]


def home_kernel(msg_ref, slot_ref, force_ref, atom_ref):
    top, rest = halves(msg_ref[...])
    slots = slot_ref[pl.ds(32, 8), :]
    high, low = slots >> 7, slots & 127

    def entry(row, values):
        return (high[row : row + 1, :], low[row : row + 1, :], values)

    def parts(c, r):
        return [top[4 * c + r : 4 * c + r + 1, :], rest[4 * c + r : 4 * c + r + 1, :]]

    grads = [sum((parts(c, r) for c in range(3)), []) for r in range(4)]
    entries = [entry(r, [-g for g in grads[r]]) for r in range(4)]
    entries += [entry(4 + r, grads[r]) for r in range(4)]
    for c, table in enumerate(spread(entries, 3)):
        force_ref[c] = table
    store_flat(atom_ref, (0,), spread([entry(4 + r, parts(3, r)) for r in range(4)], 1)[0])


def return_kernel(where_ref, own_ref, even_ref, odd_ref, slot_ref, force_in_ref, force_ref, grid_ref):
    arrange(where_ref[0], where_ref[1], own_ref, even_ref, odd_ref, grid_ref)
    slots = slot_ref[pl.ds(0, 32), :]
    high, low = slots >> 7, slots & 127
    entries = []
    for o, (dx, dy) in enumerate(DIRS):
        top, rest = halves(grid_ref[dy + 1, dx + 1])
        for r in range(4):
            values = []
            for c in range(3):
                row = slice(4 * c + r, 4 * c + r + 1)
                values += [top[row, :], rest[row, :]]
            row = slice(4 * o + r, 4 * o + r + 1)
            entries.append((high[row, :], low[row, :], values))
    for c, table in enumerate(spread(entries, 3)):
        store_flat(force_ref, (c,), force_in_ref[c] - table)


def call(kernel, outs, args, smem=(), scratch=(), hbm=False):
    many = isinstance(outs, (list, tuple))
    inside = pl.BlockSpec(memory_space=pltpu.VMEM)
    scalar = pl.BlockSpec(memory_space=pltpu.SMEM)
    outside = pl.BlockSpec(memory_space=pltpu.HBM)
    return pl.pallas_call(
        kernel,
        out_shape=outs,
        in_specs=[outside if hbm else scalar if i in smem else inside for i in range(len(args))],
        out_specs=[inside] * len(outs) if many else inside,
        scratch_shapes=list(scratch),
        compiler_params=pltpu.CompilerParams(vmem_limit_bytes=WHOLE_VMEM if hbm else VMEM_LIMIT),
    )(*args)


def exchange(to_even, to_odd, axis):
    nx, ny = lax.axis_size("gx"), lax.axis_size("gy")
    even, odd = [], []
    for i in range(nx):
        for j in range(ny):
            k, count = (i, nx) if axis == "gx" else (j, ny)
            pair = k ^ 1
            other = ((k + 1) ^ 1) - 1
            ends = other < 0 or other >= count
            if axis == "gx":
                to = (pair, j)
                far = (i, j ^ 1) if ends else (other, j)
            else:
                to = (i, pair)
                far = (i ^ 1, j) if ends else (i, other)
            even.append((i * ny + j, to[0] * ny + to[1]))
            odd.append((i * ny + j, far[0] * ny + far[1]))
    axes = ("gx", "gy")
    return lax.ppermute(to_even, axes, even), lax.ppermute(to_odd, axes, odd)


def shaped(*dims, dtype=F32):
    return jax.ShapeDtypeStruct(dims, dtype)


def edge_call(layers, args):
    return call(
        lambda *refs: edge_kernel(layers, *refs),
        shaped(16, LANES),
        args,
        smem=(0,),
        scratch=(
            pltpu.VMEM((2, layers, 128, EDGES), BF16),
            pltpu.VMEM((2, layers, 128, EDGES), BF16),
            pltpu.VMEM((256, EDGES), F32),
            pltpu.VMEM((448, EDGES), F32),
            pltpu.VMEM((256, EDGES), F32),
            pltpu.VMEM((256, EDGES), F32),
            pltpu.VMEM((layers, 192, EDGES), F32),
            pltpu.VMEM((layers, 192, EDGES), BF16),
            pltpu.VMEM((layers, 192, EDGES), F32),
            pltpu.VMEM((layers, 256, EDGES), F32),
            pltpu.VMEM((layers, 256, EDGES), F32),
        ),
    )


def per_device(
    positions,
    species,
    mig_rows,
    ghost_rows,
    edge_center,
    edge_neighbor,
    edge_blocks,
    w_radial,
    w_kind_center,
    w_kind_neigh,
    w_two,
    w_edge,
    w_env,
    w_update,
    w_out,
):
    layers = w_edge.shape[0]
    pos = positions.reshape(3, 1, SLOTS)
    kind = species.reshape(1, SLOTS)
    mig = mig_rows.reshape(8, MOVES)
    ghosts = ghost_rows.reshape(8, GHOSTS)
    centers = edge_center.reshape(1, EDGES)
    nbrs = edge_neighbor.reshape(1, EDGES)
    blocks = edge_blocks.reshape(1)
    grid = (lax.axis_size("gx"), lax.axis_size("gy"))
    place = jnp.stack([lax.axis_index("gx"), lax.axis_index("gy")]).astype(jnp.int32)

    odd_y = (place[1] & 1) > 0

    msg = call(
        send_kernel,
        shaped(24, LANES),
        (pos, kind, mig, nbrs),
        hbm=True,
        scratch=(
            pltpu.VMEM((3, 1, SLOTS), F32),
            pltpu.VMEM((1, SLOTS), jnp.int32),
            pltpu.VMEM((8, MOVES), jnp.int32),
            pltpu.VMEM((1, EDGES), jnp.int32),
            pltpu.SemaphoreType.DMA((4,)),
        ),
    )
    even, odd = exchange(msg, msg, "gx")
    column = jnp.stack([even, msg, odd])
    kept = call(keep_kernel, shaped(4, 24, LANES), (pos, kind, mig))
    even, odd = exchange(column, column, "gy")

    to_even, to_odd, same, mids, slots, arrived = call(
        lambda *refs: answer_kernel(grid, *refs),
        (
            shaped(3, 16, LANES),
            shaped(3, 16, LANES),
            shaped(3, 16, LANES),
            shaped(16, LANES),
            shaped(40, LANES, dtype=jnp.int32),
            shaped(2, 8, LANES),
        ),
        (place, column, even, odd, ghosts, centers, kept),
        smem=(0,),
        scratch=(pltpu.VMEM((3, 3, 24, LANES), F32),),
    )
    even, odd = exchange(to_even, to_odd, "gx")

    stay = kept[:3].reshape(3, 24 * LANES)[:, :SLOTS]
    late = arrived.reshape(2, 8, 2, MOVES).transpose(0, 2, 1, 3).reshape(4, 8 * MOVES)[:3]
    owned_positions = jnp.concatenate([stay, late], 1).reshape(3, 1, 1, OWNED)

    same, owned_positions = lax.optimization_barrier((same, owned_positions))
    same = same + even + odd
    down, up = same[0], same[2]
    even, odd = exchange(jnp.where(odd_y, down, up), jnp.where(odd_y, up, down), "gy")

    grad = edge_call(
        layers,
        (
            blocks, same, even, odd, mids, centers, edge_center.reshape(EDGES, 1),
            w_radial, w_kind_center, w_kind_neigh, w_two,
            w_edge.transpose(0, 2, 1), w_env.transpose(0, 2, 1), w_update,
            w_out.astype(F32).reshape(-1, 1),
        ),
    )
    even, odd = exchange(grad, grad, "gx")
    force_home, atoms = call(
        home_kernel, (shaped(3, 32, LANES), shaped(1, 1, OWNED)), (grad, slots)
    )
    column = jnp.stack([even, grad, odd])
    column, force_home, atoms = lax.optimization_barrier((column, force_home, atoms))
    even, odd = exchange(column, column, "gy")
    forces = call(
        return_kernel,
        shaped(3, 1, OWNED),
        (place, column, even, odd, slots, force_home),
        smem=(0,),
        scratch=(pltpu.VMEM((3, 3, 16, LANES), F32),),
    )
    return (owned_positions, forces.reshape(3, 1, 1, OWNED), atoms)


def solution(mesh):
    placed = (
        P(None, "gx", "gy", None),
        P("gx", "gy", None),
        P("gx", "gy", None, None),
        P("gx", "gy", None, None),
        P("gx", "gy", None),
        P("gx", "gy", None),
        P("gx", "gy"),
        P(),
        P(),
        P(),
        P(),
        P(),
        P(),
        P(),
        P(),
    )
    return jax.shard_map(
        per_device,
        mesh=mesh,
        in_specs=placed,
        out_specs=(P(None, "gx", "gy", None), P(None, "gx", "gy", None), P("gx", "gy", None)),
        check_vma=False,
    )
```

```python
import math

import jax
import jax.numpy as jnp
from jax import lax
from jax.experimental import pallas as pl
from jax.experimental.pallas import tpu as pltpu
from jax.sharding import PartitionSpec as P

CUTOFF = 6.0
SOFTENING = 0.01
BASIS_WIDTH = 0.8
ENV_SCALE = 0.3
ROOT3 = math.sqrt(3.0)
ROOT5 = math.sqrt(5.0)
ROOT15 = math.sqrt(15.0)
DIRS = ((-1, -1), (-1, 0), (-1, 1), (0, -1), (0, 1), (1, -1), (1, 0), (1, 1))
SLOTS = 2940
MOVES = 64
OWNED = 3452
GHOSTS = 1260
EDGES = 512
LANES = 128
KEPT_ROWS = 23
F32 = jnp.float32
BF16 = jnp.bfloat16
VMEM_LIMIT = 48 * 1024 * 1024
WHOLE_VMEM = 64 * 1024 * 1024

NN = (((1,), (0,)), ((), ()))
NT = (((1,), (1,)), ((), ()))
TN = (((0,), (0,)), ((), ()))


def mm(a, b, dims=NN):
    return lax.dot_general(a, b, dims, preferred_element_type=F32)


def split(x):
    top = x.astype(BF16)
    return top, (x - top.astype(F32)).astype(BF16)


def halves(x):
    top = x.astype(BF16).astype(F32)
    return top, x - top


def column_of(row):
    return jnp.broadcast_to(row, (8, row.shape[1])).T[:, :1]


def lane_pick(row, low):
    table = jnp.broadcast_to(row, low.shape)
    return jnp.take_along_axis(table, low, axis=1, mode="promise_in_bounds")


def full_row(ref, lead, start, size):
    stop = min(start + LANES, size)
    piece = ref[lead + (slice(None), slice(start, stop))]
    if stop - start < LANES:
        pad = jnp.zeros((1, LANES - (stop - start)), piece.dtype)
        piece = jnp.concatenate([piece, pad], axis=1)
    return piece


def payload_row(pos_ref, kind_ref, chan, h):
    if chan < 3:
        return full_row(pos_ref, (chan,), h * LANES, SLOTS)
    return full_row(kind_ref, (), h * LANES, SLOTS).astype(F32)


def send_kernel(pos_hbm, kind_hbm, mig_hbm, nbr_hbm, msg_ref, pos_ref, kind_ref, mig_ref, nbr_ref, sems):
    copies = [
        pltpu.make_async_copy(a, b, sems.at[i])
        for i, (a, b) in enumerate(
            ((mig_hbm, mig_ref), (nbr_hbm, nbr_ref), (kind_hbm, kind_ref), (pos_hbm, pos_ref))
        )
    ]
    for copy in copies:
        copy.start()
    copies[0].wait()
    rows = mig_ref[...]
    rows = jnp.concatenate([rows, jnp.full((8, LANES - MOVES), -1, jnp.int32)], axis=1)
    high, low = rows >> 7, rows & 127
    copies[1].wait()
    for r in range(4):
        msg_ref[pl.ds(16 + r, 1), :] = nbr_ref[:, r * LANES : (r + 1) * LANES].astype(F32)
    msg_ref[pl.ds(20, 4), :] = jnp.zeros((4, LANES), F32)
    copies[2].wait()
    copies[3].wait()
    picked = [jnp.zeros((8, LANES), F32) for _ in range(4)]
    for h in range(KEPT_ROWS):
        here = high == h
        for c in range(4):
            got = lane_pick(payload_row(pos_ref, kind_ref, c, h), low)
            picked[c] = jnp.where(here, got, picked[c])
    for p in range(2):
        msg_ref[pl.ds(8 * p, 8), :] = picked[2 * p] + pltpu.roll(picked[2 * p + 1], MOVES, 1)


def ghost_slots(pair, listed, inside, ghost_ref):
    parts = []
    for d in pair:
        rank = listed[d].astype(jnp.int32) - (OWNED + GHOSTS * (7 - d))
        ok = (rank >= 0) & (rank < GHOSTS) & (inside[d] > 0)
        parts.append(jnp.where(ok, rank, -1))
    rank = jnp.concatenate(parts, axis=0)
    high, low = rank >> 7, rank & 127
    slot = jnp.full((8, LANES), -1, jnp.int32)
    upper = lax.broadcasted_iota(jnp.int32, (8, LANES), 0) < 4
    for h in range(10):
        stop = min((h + 1) * LANES, GHOSTS)
        rows = []
        for d in pair:
            row = ghost_ref[pl.ds(d, 1), h * LANES : stop]
            if stop - h * LANES < LANES:
                pad = jnp.full((1, LANES - (stop - h * LANES)), -1, jnp.int32)
                row = jnp.concatenate([row, pad], axis=1)
            rows.append(jnp.broadcast_to(row, (8, LANES)))
        table = jnp.where(upper, rows[0], rows[1])
        got = jnp.take_along_axis(table, low, axis=1, mode="promise_in_bounds")
        slot = jnp.where(high == h, got, slot)
    return jnp.where(slot >= OWNED, -1, slot)


def kept_values(slot, kept_ref):
    high = jnp.where(slot < SLOTS, slot >> 7, -1)
    low = slot & 127
    found = [jnp.zeros((8, LANES), F32) for _ in range(4)]
    for h in range(KEPT_ROWS):
        here = high == h
        for c in range(4):
            got = lane_pick(kept_ref[c, pl.ds(h, 1), :], low)
            found[c] = jnp.where(here, got, found[c])
    return found


def late_values(slot, arrive_ref, found):
    late = slot - SLOTS
    high = jnp.where(late >= 0, late >> 6, -1)
    low = late & 63
    found = list(found)
    for h in range(8):
        here = high == h
        for c in range(4):
            got = lane_pick(arrive_ref[c // 2, pl.ds(h, 1), :], low + MOVES if c % 2 else low)
            found[c] = jnp.where(here, got, found[c])
    return found


def on_grid(grid, where_ref):
    nx, ny = grid
    ix, iy = where_ref[0], where_ref[1]
    inside = []
    for dx, dy in DIRS:
        ok = (ix + dx >= 0) & (ix + dx < nx) & (iy + dy >= 0) & (iy + dy < ny)
        inside.append(ok.astype(jnp.int32))
    return inside


def keep_kernel(
    grid, where_ref, pos_ref, kind_ref, mig_ref, column_ref, ghost_ref, center_ref,
    kept_ref, early_ref, early_slot_ref,
):
    rows = mig_ref[...]
    rows = jnp.concatenate([rows, jnp.full((8, LANES - MOVES), -1, jnp.int32)], axis=1)
    high, low = rows >> 7, rows & 127
    sub32 = lax.broadcasted_iota(jnp.int32, (32, LANES), 0)
    sub128 = lax.broadcasted_iota(jnp.int32, (LANES, LANES), 0)
    left = jnp.zeros((32, LANES), F32)
    for k in range(8):
        a = (sub32 == high[k : k + 1, :]).astype(F32).astype(BF16)
        b = (sub128 == low[k : k + 1, :]).astype(F32).astype(BF16)
        left = left + mm(a, b, NT)
    stay = left < 0.5
    for c in range(4):
        table = jnp.concatenate(
            [payload_row(pos_ref, kind_ref, c, h) for h in range(KEPT_ROWS)]
            + [jnp.zeros((1, LANES), F32)],
            axis=0,
        )
        kept_ref[c] = jnp.where(stay[:24, :], table, 0.0)
    odd_x = where_ref[0] & 1
    listed = {
        1: column_ref[2 - 2 * odd_x, pl.ds(16, 4), :],
        6: column_ref[2 * odd_x, pl.ds(16, 4), :],
    }
    near = column_ref[1, pl.ds(16, 4), :].astype(jnp.int32)
    core = [center_ref[:, r * LANES : (r + 1) * LANES] for r in range(4)]
    asked = (
        ghost_slots((1, 6), listed, on_grid(grid, where_ref), ghost_ref),
        jnp.concatenate([jnp.where(near < OWNED, near, -1)] + core, axis=0),
    )
    for g, slot in enumerate(asked):
        early_slot_ref[pl.ds(8 * g, 8), :] = slot
        for c, found in enumerate(kept_values(slot, kept_ref)):
            early_ref[g, c] = found


def arrange(ix, iy, own_ref, even_ref, odd_ref, grid_ref):
    odd_x, odd_y = ix & 1, iy & 1
    for dx in (-1, 0, 1):
        block = {-1: 2 - 2 * odd_x, 0: 1, 1: 2 * odd_x}[dx]
        even, odd = even_ref[block], odd_ref[block]
        grid_ref[0, dx + 1] = jnp.where(odd_y > 0, even, odd)
        grid_ref[1, dx + 1] = own_ref[block]
        grid_ref[2, dx + 1] = jnp.where(odd_y > 0, odd, even)


def answer_kernel(
    grid, where_ref, own_ref, even_ref, odd_ref, ghost_ref, kept_ref, early_ref, early_slot_ref,
    to_even_ref, to_odd_ref, same_ref, center_out, slot_ref, arrive_ref, grid_ref,
):
    ix, iy = where_ref[0], where_ref[1]
    arrange(ix, iy, own_ref, even_ref, odd_ref, grid_ref)
    inside = on_grid(grid, where_ref)
    listed = []
    for k, (dx, dy) in enumerate(DIRS):
        listed.append(grid_ref[dy + 1, dx + 1, pl.ds(16, 4), :])
        for p in range(2):
            row = grid_ref[dy + 1, dx + 1, pl.ds(8 * p + 7 - k, 1), :]
            arrive_ref[p, pl.ds(k, 1), :] = row * inside[k].astype(F32)
    values = {}
    for pair in ((1, 6), (8, 9), (0, 2), (5, 7), (3, 4)):
        if pair in ((1, 6), (8, 9)):
            g = 0 if pair == (1, 6) else 1
            slot = early_slot_ref[pl.ds(8 * g, 8), :]
            found = [early_ref[g, c] for c in range(4)]
        else:
            slot = ghost_slots(pair, listed, inside, ghost_ref)
            found = kept_values(slot, kept_ref)
        found = late_values(slot, arrive_ref, found)
        for half, d in enumerate(pair):
            rows = slice(4 * half, 4 * half + 4)
            slot_ref[pl.ds(4 * d, 4), :] = slot[rows, :]
            values[d] = [found[c][rows, :] for c in range(4)]
    flip = (ix & 1) > 0
    for c in range(4):
        rows = pl.ds(4 * c, 4)
        center_out[rows, :] = values[9][c]
        for y, (lower, mid, upper) in enumerate(((0, 3, 5), (1, 8, 6), (2, 4, 7))):
            same_ref[y, rows, :] = values[mid][c]
            to_even_ref[y, rows, :] = jnp.where(flip, values[lower][c], values[upper][c])
            to_odd_ref[y, rows, :] = jnp.where(flip, values[upper][c], values[lower][c])


def edge_kernel(
    layers,
    blocks_ref, same_ref, below_ref, above_ref, center_ref, core_row_ref,
    w_rad_ref, w_kc_ref, w_kn_ref, w_two_ref, w_edge_t_ref, w_env_t_ref, w_up_ref, w_out_ref,
    msg_ref,
    lhs_ref, rhs_ref, back_ref, joined_ref, latent_ref, d_latent_ref, edge_mix_ref, env_mix_ref,
    pooled_ref, act_ref, slope_ref,
):
    near = same_ref[1] + below_ref[...] + above_ref[...]
    mid = center_ref[...]

    def flat(rows, c):
        return jnp.concatenate([rows[4 * c + r : 4 * c + r + 1, :] for r in range(4)], axis=1)

    delta = [flat(near, c) - flat(mid, c) for c in range(3)]
    kind_n, kind_c = flat(near, 3), flat(mid, 3)
    radius = jnp.sqrt(delta[0] * delta[0] + delta[1] * delta[1] + delta[2] * delta[2] + SOFTENING)
    inv_radius = 1.0 / radius
    block = lax.broadcasted_iota(jnp.int32, (1, EDGES), 1) >> 7
    live = (block < blocks_ref[0]) & (kind_c > 0.5) & (kind_n > 0.5)
    live = jnp.where(live, 1.0, 0.0)
    ramp = jnp.maximum(0.0, 1.0 - radius * radius / (CUTOFF * CUTOFF))
    envelope = live * ramp * ramp
    ux, uy, uz = (d * (1.0 / CUTOFF) for d in delta)
    sph = [
        ROOT3 * ux,
        ROOT3 * uy,
        ROOT3 * uz,
        ROOT15 * ux * uy,
        ROOT15 * uy * uz,
        ROOT15 * ux * uz,
        (0.5 * ROOT5) * (2.0 * uz * uz - ux * ux - uy * uy),
        (0.5 * ROOT15) * (ux * ux - uy * uy),
    ]
    q8 = lax.broadcasted_iota(jnp.int32, (8, EDGES), 0)
    shift = radius - q8.astype(F32) * (CUTOFF / 7.0)
    radial = jnp.exp(-(shift * shift) * (1.0 / (BASIS_WIDTH * BASIS_WIDTH)))
    ids = (q8 & 3) + 1
    kinds = jnp.where(q8 < 4, kind_c, kind_n)
    onehot = jnp.where(kinds == ids.astype(F32), 1.0, 0.0)
    core_row = core_row_ref[...].astype(F32)
    same_center = column_of(core_row) == core_row
    zero_row = jnp.zeros((1, EDGES), F32)

    def gram(rows):
        top, rest = [], []
        for row in rows:
            a, b = split(row)
            top.append(a.astype(F32))
            rest.append(b.astype(F32))
        fill = [jnp.zeros((LANES - 3 * len(rows), EDGES), F32)]
        a = jnp.concatenate(top + top + rest + fill, axis=0).astype(BF16)
        b = jnp.concatenate(top + rest + top + fill, axis=0).astype(BF16)
        return jnp.where(same_center, mm(a, b, TN), 0.0).astype(BF16)

    grams = [jnp.where(same_center, 1.0, 0.0).astype(BF16), gram(sph[:3]), gram(sph[3:])]

    w_top, w_rest = halves(
        jnp.concatenate([w_rad_ref[...], w_kc_ref[...], w_kn_ref[...]], axis=0)
    )
    f_top, f_rest = halves(jnp.concatenate([radial, onehot], axis=0))
    w_in = jnp.concatenate([w_top, w_rest, w_top, jnp.zeros((LANES - 48, 256), F32)], axis=0)
    feats = jnp.concatenate([f_top, f_top, f_rest, jnp.zeros((LANES - 48, EDGES), F32)], axis=0)
    pre = mm(w_in.astype(BF16), feats.astype(BF16), TN)

    def sigmoid(x):
        return 0.5 * jnp.tanh(0.5 * x) + 0.5

    gate0 = sigmoid(pre)
    hidden = (pre * gate0).astype(BF16)
    slope0 = gate0 * (1.0 + pre * (1.0 - gate0))
    two = mm(w_two_ref[...], hidden, TN)
    gate1 = sigmoid(two)
    act1 = two * gate1
    slope1 = gate1 * (1.0 + two * (1.0 - gate1))
    latent_ref[...] = act1 * envelope

    def forward(t, carry):
        latent = latent_ref[...]
        latent_b = latent.astype(BF16)
        edge_mix = mm(w_edge_t_ref[t], latent_b)
        env_mix = mm(w_env_t_ref[t], latent_b).astype(BF16)
        pooled = jnp.concatenate(
            [mm(env_mix[64 * l : 64 * l + 64, :], grams[l]) for l in range(3)], axis=0
        ) * ENV_SCALE
        invariants = (edge_mix * pooled).astype(BF16)
        update = mm(w_up_ref[t], jnp.concatenate([latent_b, invariants], axis=0), TN)
        gate = sigmoid(update)
        act = update * gate
        edge_mix_ref[t] = edge_mix
        env_mix_ref[t] = env_mix
        pooled_ref[t] = pooled
        act_ref[t] = act
        slope_ref[t] = gate * (1.0 + update * (1.0 - gate))
        latent_ref[...] = latent + act * envelope
        return carry

    lax.fori_loop(0, layers, forward, 0)
    w_out = column_of(w_out_ref[...].astype(F32))
    read = jnp.sum(latent_ref[...].astype(BF16).astype(F32) * w_out, axis=0, keepdims=True)
    energy = envelope * read
    d_latent_ref[...] = (w_out * envelope).astype(BF16).astype(F32)

    def backward(s, d_env):
        t = layers - 1 - s
        d_latent = d_latent_ref[...]
        d_env = d_env + jnp.sum(d_latent * act_ref[t], axis=0, keepdims=True)
        d_update = (d_latent * envelope * slope_ref[t]).astype(BF16)
        joined_ref[...] = mm(w_up_ref[t], d_update)
        d_inv = joined_ref[pl.ds(256, 192), :]
        d_edge_mix = (d_inv * pooled_ref[t]).astype(BF16)
        d_pooled = (d_inv * edge_mix_ref[t] * ENV_SCALE).astype(BF16)
        d_env_mix = jnp.concatenate(
            [mm(d_pooled[64 * l : 64 * l + 64, :], grams[l]) for l in range(3)], axis=0
        ).astype(BF16)
        for l in range(1, 3):
            mix_l = env_mix_ref[t, pl.ds(64 * l, 64), :]
            pool_l = d_pooled[64 * l : 64 * l + 64, :]
            lhs_ref[l - 1, t] = jnp.concatenate([pool_l, mix_l], axis=0)
            rhs_ref[l - 1, t] = jnp.concatenate([mix_l, pool_l], axis=0)
        back_ref[...] = mm(
            jnp.concatenate([w_edge_t_ref[t], w_env_t_ref[t]], axis=0),
            jnp.concatenate([d_edge_mix, d_env_mix], axis=0),
            TN,
        )
        d_latent_ref[...] = d_latent + joined_ref[pl.ds(0, 256), :] + back_ref[...]
        return d_env

    d_env = lax.fori_loop(0, layers, backward, read)
    d_latent = d_latent_ref[...]
    d_env = d_env + jnp.sum(d_latent * act1, axis=0, keepdims=True)
    d_two = (d_latent * envelope * slope1).astype(BF16)
    d_pre = mm(w_two_ref[...], d_two) * slope0
    w_back = jnp.concatenate([w_top[:8, :], w_rest[:8, :]], axis=0).astype(BF16)
    d_radial = mm(w_back, d_pre.astype(BF16))
    d_radial = d_radial[:8, :] + d_radial[8:, :]
    d_radius = jnp.sum(
        d_radial * radial * shift, axis=0, keepdims=True
    ) * (-2.0 / (BASIS_WIDTH * BASIS_WIDTH))
    d_radius = d_radius - d_env * live * ramp * radius * (4.0 / (CUTOFF * CUTOFF))

    def both(ref, l):
        return jnp.concatenate([ref[l - 1, t] for t in range(layers)], axis=0)

    d_sph = []
    for l, rows in ((1, sph[:3]), (2, sph[3:])):
        pairs = jnp.where(same_center, mm(both(lhs_ref, l), both(rhs_ref, l), TN), 0.0)
        fill = [zero_row] * (8 - len(rows))
        y_top, y_rest = halves(jnp.concatenate(list(rows) + fill, axis=0))
        got = mm(jnp.concatenate([y_top, y_rest], axis=0).astype(BF16), pairs.astype(BF16))
        got = got[:8, :] + got[8:, :]
        d_sph += [got[i : i + 1, :] for i in range(len(rows))]
    d1, d2, d3, d4, d5, d6, d7, d8 = d_sph
    du = [
        ROOT3 * d1 + ROOT15 * (uy * d4 + uz * d6 + ux * d8) - ROOT5 * ux * d7,
        ROOT3 * d2 + ROOT15 * (ux * d4 + uz * d5 - uy * d8) - ROOT5 * uy * d7,
        ROOT3 * d3 + ROOT15 * (uy * d5 + ux * d6) + (2.0 * ROOT5) * uz * d7,
    ]
    scale = d_radius * inv_radius
    for c in range(3):
        grad = scale * delta[c] + du[c] * (1.0 / CUTOFF)
        for r in range(4):
            msg_ref[pl.ds(4 * c + r, 1), :] = grad[:, r * LANES : (r + 1) * LANES]
    for r in range(4):
        msg_ref[pl.ds(12 + r, 1), :] = energy[:, r * LANES : (r + 1) * LANES]


def spread(entries, chans):
    sub32 = lax.broadcasted_iota(jnp.int32, (32, LANES), 0)
    sub128 = lax.broadcasted_iota(jnp.int32, (LANES, LANES), 0)
    pieces = len(entries[0][2]) // chans
    total = jnp.zeros((pieces * chans * 32, LANES), F32)
    for first in range(0, len(entries), 2):
        a_parts, b_parts = [], []
        for high, low, values in entries[first : first + 2]:
            here = sub32 == high
            a_parts.append(jnp.concatenate([jnp.where(here, v, 0.0) for v in values], axis=0))
            b_parts.append(jnp.where(sub128 == low, 1.0, 0.0))
        a = jnp.concatenate(a_parts, axis=1).astype(BF16)
        b = jnp.concatenate(b_parts, axis=1).astype(BF16)
        total = total + mm(a, b, NT)
    tables = [total[32 * i : 32 * i + 32, :] for i in range(pieces * chans)]
    return [sum(tables[c * pieces + 1 : (c + 1) * pieces], tables[c * pieces]) for c in range(chans)]


def store_flat(ref, lead, table):
    for h in range(27):
        stop = min((h + 1) * LANES, OWNED)
        ref[lead + (slice(None), slice(h * LANES, stop))] = table[h : h + 1, : stop - h * LANES]


def ghost_entries(slot_ref, block_of, wanted):
    slots = slot_ref[pl.ds(0, 32), :]
    high, low = slots >> 7, slots & 127
    entries = []
    for o, (dx, dy) in enumerate(DIRS):
        if (dy == 0) != wanted:
            continue
        top, rest = halves(block_of(dx, dy))
        for r in range(4):
            values = []
            for c in range(3):
                row = slice(4 * c + r, 4 * c + r + 1)
                values += [top[row, :], rest[row, :]]
            row = slice(4 * o + r, 4 * o + r + 1)
            entries.append((high[row, :], low[row, :], values))
    return entries


def home_kernel(where_ref, column_ref, slot_ref, force_ref, atom_ref):
    top, rest = halves(column_ref[1])
    slots = slot_ref[pl.ds(32, 8), :]
    high, low = slots >> 7, slots & 127
    odd_x = where_ref[0] & 1

    def entry(row, values):
        return (high[row : row + 1, :], low[row : row + 1, :], values)

    def parts(c, r):
        return [top[4 * c + r : 4 * c + r + 1, :], rest[4 * c + r : 4 * c + r + 1, :]]

    def block_of(dx, dy):
        return column_ref[2 - 2 * odd_x if dx < 0 else 2 * odd_x]

    grads = [sum((parts(c, r) for c in range(3)), []) for r in range(4)]
    entries = [entry(r, [-g for g in grads[r]]) for r in range(4)]
    entries += [entry(4 + r, grads[r]) for r in range(4)]
    ghosts = [(h, l, [-v for v in values]) for h, l, values in ghost_entries(slot_ref, block_of, True)]
    for c, table in enumerate(spread(entries + ghosts, 3)):
        force_ref[c] = table
    store_flat(atom_ref, (0,), spread([entry(4 + r, parts(3, r)) for r in range(4)], 1)[0])


def return_kernel(where_ref, even_ref, odd_ref, slot_ref, force_in_ref, force_ref):
    odd_x, odd_y = where_ref[0] & 1, where_ref[1] & 1

    def block_of(dx, dy):
        block = {-1: 2 - 2 * odd_x, 0: 1, 1: 2 * odd_x}[dx]
        use_even = (odd_y > 0) if dy < 0 else (odd_y == 0)
        return jnp.where(use_even, even_ref[block], odd_ref[block])

    for c, table in enumerate(spread(ghost_entries(slot_ref, block_of, False), 3)):
        store_flat(force_ref, (c,), force_in_ref[c] - table)


def call(kernel, outs, args, smem=(), scratch=(), hbm=False):
    many = isinstance(outs, (list, tuple))
    inside = pl.BlockSpec(memory_space=pltpu.VMEM)
    scalar = pl.BlockSpec(memory_space=pltpu.SMEM)
    outside = pl.BlockSpec(memory_space=pltpu.HBM)
    return pl.pallas_call(
        kernel,
        out_shape=outs,
        in_specs=[outside if hbm else scalar if i in smem else inside for i in range(len(args))],
        out_specs=[inside] * len(outs) if many else inside,
        scratch_shapes=list(scratch),
        compiler_params=pltpu.CompilerParams(vmem_limit_bytes=WHOLE_VMEM if hbm else VMEM_LIMIT),
    )(*args)


def exchange(to_even, to_odd, axis):
    nx, ny = lax.axis_size("gx"), lax.axis_size("gy")
    even, odd = [], []
    for i in range(nx):
        for j in range(ny):
            k, count = (i, nx) if axis == "gx" else (j, ny)
            pair = k ^ 1
            other = ((k + 1) ^ 1) - 1
            ends = other < 0 or other >= count
            if axis == "gx":
                to = (pair, j)
                far = (i, j ^ 1) if ends else (other, j)
            else:
                to = (i, pair)
                far = (i ^ 1, j) if ends else (i, other)
            even.append((i * ny + j, to[0] * ny + to[1]))
            odd.append((i * ny + j, far[0] * ny + far[1]))
    axes = ("gx", "gy")
    b = lax.optimization_barrier((lax.ppermute(to_odd, axes, odd), lax.ppermute(to_even, axes, even)))
    return b[1], b[0]


def shaped(*dims, dtype=F32):
    return jax.ShapeDtypeStruct(dims, dtype)


def edge_call(layers, args):
    return call(
        lambda *refs: edge_kernel(layers, *refs),
        shaped(16, LANES),
        args,
        smem=(0,),
        scratch=(
            pltpu.VMEM((2, layers, 128, EDGES), BF16),
            pltpu.VMEM((2, layers, 128, EDGES), BF16),
            pltpu.VMEM((256, EDGES), F32),
            pltpu.VMEM((448, EDGES), F32),
            pltpu.VMEM((256, EDGES), F32),
            pltpu.VMEM((256, EDGES), F32),
            pltpu.VMEM((layers, 192, EDGES), F32),
            pltpu.VMEM((layers, 192, EDGES), BF16),
            pltpu.VMEM((layers, 192, EDGES), F32),
            pltpu.VMEM((layers, 256, EDGES), F32),
            pltpu.VMEM((layers, 256, EDGES), F32),
        ),
    )


def per_device(
    positions,
    species,
    mig_rows,
    ghost_rows,
    edge_center,
    edge_neighbor,
    edge_blocks,
    w_radial,
    w_kind_center,
    w_kind_neigh,
    w_two,
    w_edge,
    w_env,
    w_update,
    w_out,
):
    layers = w_edge.shape[0]
    pos = positions.reshape(3, 1, SLOTS)
    kind = species.reshape(1, SLOTS)
    mig = mig_rows.reshape(8, MOVES)
    ghosts = ghost_rows.reshape(8, GHOSTS)
    centers = edge_center.reshape(1, EDGES)
    nbrs = edge_neighbor.reshape(1, EDGES)
    blocks = edge_blocks.reshape(1)
    grid = (lax.axis_size("gx"), lax.axis_size("gy"))
    place = jnp.stack([lax.axis_index("gx"), lax.axis_index("gy")]).astype(jnp.int32)

    odd_y = (place[1] & 1) > 0

    msg = call(
        send_kernel,
        shaped(24, LANES),
        (pos, kind, mig, nbrs),
        hbm=True,
        scratch=(
            pltpu.VMEM((3, 1, SLOTS), F32),
            pltpu.VMEM((1, SLOTS), jnp.int32),
            pltpu.VMEM((8, MOVES), jnp.int32),
            pltpu.VMEM((1, EDGES), jnp.int32),
            pltpu.SemaphoreType.DMA((4,)),
        ),
    )
    even, odd = exchange(msg, msg, "gx")
    column = jnp.stack([even, msg, odd])
    kept, early, early_slots = call(
        lambda *refs: keep_kernel(grid, *refs),
        (
            shaped(4, 24, LANES),
            shaped(2, 4, 8, LANES),
            shaped(16, LANES, dtype=jnp.int32),
        ),
        (place, pos, kind, mig, column, ghosts, centers),
        smem=(0,),
    )
    even, odd = exchange(column, column, "gy")

    to_even, to_odd, same, mids, slots, arrived = call(
        lambda *refs: answer_kernel(grid, *refs),
        (
            shaped(3, 16, LANES),
            shaped(3, 16, LANES),
            shaped(3, 16, LANES),
            shaped(16, LANES),
            shaped(40, LANES, dtype=jnp.int32),
            shaped(2, 8, LANES),
        ),
        (place, column, even, odd, ghosts, kept, early, early_slots),
        smem=(0,),
        scratch=(pltpu.VMEM((3, 3, 24, LANES), F32),),
    )
    even, odd = exchange(to_even, to_odd, "gx")

    stay = kept[:3].reshape(3, 24 * LANES)[:, :SLOTS]
    late = arrived.reshape(2, 8, 2, MOVES).transpose(0, 2, 1, 3).reshape(4, 8 * MOVES)[:3]
    owned_positions = jnp.concatenate([stay, late], 1).reshape(3, 1, 1, OWNED)

    same = same + even + odd
    down, up = same[0], same[2]
    even, odd = exchange(jnp.where(odd_y, down, up), jnp.where(odd_y, up, down), "gy")

    mids, owned_positions = lax.optimization_barrier((mids, owned_positions))
    grad = edge_call(
        layers,
        (
            blocks, same, even, odd, mids, centers,
            w_radial, w_kind_center, w_kind_neigh, w_two,
            w_edge.transpose(0, 2, 1), w_env.transpose(0, 2, 1), w_update,
            w_out.reshape(1, -1),
        ),
    )
    even, odd = exchange(grad, grad, "gx")
    column = jnp.stack([even, grad, odd])
    force_home, atoms = call(
        home_kernel, (shaped(3, 32, LANES), shaped(1, 1, OWNED)), (place, column, slots), smem=(0,)
    )
    even, odd = exchange(column, column, "gy")
    forces = call(
        return_kernel, shaped(3, 1, OWNED), (place, even, odd, slots, force_home), smem=(0,)
    )
    return (owned_positions, forces.reshape(3, 1, 1, OWNED), atoms)


def solution(mesh):
    placed = (
        P(None, "gx", "gy", None),
        P("gx", "gy", None),
        P("gx", "gy", None, None),
        P("gx", "gy", None, None),
        P("gx", "gy", None),
        P("gx", "gy", None),
        P("gx", "gy"),
        P(),
        P(),
        P(),
        P(),
        P(),
        P(),
        P(),
        P(),
    )
    return jax.shard_map(
        per_device,
        mesh=mesh,
        in_specs=placed,
        out_specs=(P(None, "gx", "gy", None), P(None, "gx", "gy", None), P("gx", "gy", None)),
        check_vma=False,
    )
```

```python
import math

import jax
import jax.numpy as jnp
from jax import lax
from jax.experimental import pallas as pl
from jax.experimental.pallas import tpu as pltpu
from jax.sharding import PartitionSpec as P

CUTOFF = 6.0
SOFTENING = 0.01
BASIS_WIDTH = 0.8
ENV_SCALE = 0.3
ROOT3 = math.sqrt(3.0)
ROOT5 = math.sqrt(5.0)
ROOT15 = math.sqrt(15.0)
DIRS = ((-1, -1), (-1, 0), (-1, 1), (0, -1), (0, 1), (1, -1), (1, 0), (1, 1))
SLOTS = 2940
MOVES = 64
OWNED = 3452
GHOSTS = 1260
EDGES = 512
LANES = 128
KEPT_ROWS = 23
F32 = jnp.float32
BF16 = jnp.bfloat16
VMEM_LIMIT = 48 * 1024 * 1024
WHOLE_VMEM = 64 * 1024 * 1024

NN = (((1,), (0,)), ((), ()))
NT = (((1,), (1,)), ((), ()))
TN = (((0,), (0,)), ((), ()))


def mm(a, b, dims=NN):
    return lax.dot_general(a, b, dims, preferred_element_type=F32)


def split(x):
    top = x.astype(BF16)
    return top, (x - top.astype(F32)).astype(BF16)


def halves(x):
    top = x.astype(BF16).astype(F32)
    return top, x - top


def column_of(row):
    return jnp.broadcast_to(row, (8, row.shape[1])).T[:, :1]


def lane_pick(row, low):
    table = jnp.broadcast_to(row, low.shape)
    return jnp.take_along_axis(table, low, axis=1, mode="promise_in_bounds")


def full_row(ref, lead, start, size):
    stop = min(start + LANES, size)
    piece = ref[lead + (slice(None), slice(start, stop))]
    if stop - start < LANES:
        pad = jnp.zeros((1, LANES - (stop - start)), piece.dtype)
        piece = jnp.concatenate([piece, pad], axis=1)
    return piece


def payload_row(pos_ref, kind_ref, chan, h):
    if chan < 3:
        return full_row(pos_ref, (chan,), h * LANES, SLOTS)
    return full_row(kind_ref, (), h * LANES, SLOTS).astype(F32)


def send_kernel(pos_hbm, kind_hbm, mig_hbm, nbr_hbm, msg_ref, pos_ref, kind_ref, mig_ref, nbr_ref, sems):
    copies = [
        pltpu.make_async_copy(a, b, sems.at[i])
        for i, (a, b) in enumerate(
            ((mig_hbm, mig_ref), (nbr_hbm, nbr_ref), (kind_hbm, kind_ref), (pos_hbm, pos_ref))
        )
    ]
    for copy in copies:
        copy.start()
    copies[0].wait()
    rows = mig_ref[...]
    rows = jnp.concatenate([rows, jnp.full((8, LANES - MOVES), -1, jnp.int32)], axis=1)
    high, low = rows >> 7, rows & 127
    copies[1].wait()
    for r in range(4):
        msg_ref[pl.ds(16 + r, 1), :] = nbr_ref[:, r * LANES : (r + 1) * LANES].astype(F32)
    msg_ref[pl.ds(20, 4), :] = jnp.zeros((4, LANES), F32)
    copies[2].wait()
    copies[3].wait()
    picked = [jnp.zeros((8, LANES), F32) for _ in range(4)]
    for h in range(KEPT_ROWS):
        here = high == h
        for c in range(4):
            got = lane_pick(payload_row(pos_ref, kind_ref, c, h), low)
            picked[c] = jnp.where(here, got, picked[c])
    for p in range(2):
        msg_ref[pl.ds(8 * p, 8), :] = picked[2 * p] + pltpu.roll(picked[2 * p + 1], MOVES, 1)


def ghost_slots(pair, listed, inside, ghost_ref):
    parts = []
    for d in pair:
        rank = listed[d].astype(jnp.int32) - (OWNED + GHOSTS * (7 - d))
        ok = (rank >= 0) & (rank < GHOSTS) & (inside[d] > 0)
        parts.append(jnp.where(ok, rank, -1))
    rank = jnp.concatenate(parts, axis=0)
    high, low = rank >> 7, rank & 127
    slot = jnp.full((8, LANES), -1, jnp.int32)
    upper = lax.broadcasted_iota(jnp.int32, (8, LANES), 0) < 4
    for h in range(10):
        stop = min((h + 1) * LANES, GHOSTS)
        rows = []
        for d in pair:
            row = ghost_ref[pl.ds(d, 1), h * LANES : stop]
            if stop - h * LANES < LANES:
                pad = jnp.full((1, LANES - (stop - h * LANES)), -1, jnp.int32)
                row = jnp.concatenate([row, pad], axis=1)
            rows.append(jnp.broadcast_to(row, (8, LANES)))
        table = jnp.where(upper, rows[0], rows[1])
        got = jnp.take_along_axis(table, low, axis=1, mode="promise_in_bounds")
        slot = jnp.where(high == h, got, slot)
    return jnp.where(slot >= OWNED, -1, slot)


def kept_values(slot, kept_ref):
    high = jnp.where(slot < SLOTS, slot >> 7, -1)
    low = slot & 127
    found = [jnp.zeros((8, LANES), F32) for _ in range(4)]
    for h in range(KEPT_ROWS):
        here = high == h
        for c in range(4):
            got = lane_pick(kept_ref[c, pl.ds(h, 1), :], low)
            found[c] = jnp.where(here, got, found[c])
    return found


def late_values(slot, arrive_ref, found):
    late = slot - SLOTS
    high = jnp.where(late >= 0, late >> 6, -1)
    low = late & 63
    found = list(found)
    for h in range(8):
        here = high == h
        for c in range(4):
            got = lane_pick(arrive_ref[c // 2, pl.ds(h, 1), :], low + MOVES if c % 2 else low)
            found[c] = jnp.where(here, got, found[c])
    return found


def on_grid(grid, where_ref):
    nx, ny = grid
    ix, iy = where_ref[0], where_ref[1]
    inside = []
    for dx, dy in DIRS:
        ok = (ix + dx >= 0) & (ix + dx < nx) & (iy + dy >= 0) & (iy + dy < ny)
        inside.append(ok.astype(jnp.int32))
    return inside


def keep_kernel(
    grid, where_ref, pos_ref, kind_ref, mig_ref, column_ref, ghost_ref, center_ref,
    kept_ref, early_ref, early_slot_ref,
):
    rows = mig_ref[...]
    rows = jnp.concatenate([rows, jnp.full((8, LANES - MOVES), -1, jnp.int32)], axis=1)
    high, low = rows >> 7, rows & 127
    sub32 = lax.broadcasted_iota(jnp.int32, (32, LANES), 0)
    sub128 = lax.broadcasted_iota(jnp.int32, (LANES, LANES), 0)
    left = jnp.zeros((32, LANES), F32)
    for k in range(8):
        a = (sub32 == high[k : k + 1, :]).astype(F32).astype(BF16)
        b = (sub128 == low[k : k + 1, :]).astype(F32).astype(BF16)
        left = left + mm(a, b, NT)
    stay = left < 0.5
    for c in range(4):
        table = jnp.concatenate(
            [payload_row(pos_ref, kind_ref, c, h) for h in range(KEPT_ROWS)]
            + [jnp.zeros((1, LANES), F32)],
            axis=0,
        )
        kept_ref[c] = jnp.where(stay[:24, :], table, 0.0)
    odd_x = where_ref[0] & 1
    listed = {
        1: column_ref[2 - 2 * odd_x, pl.ds(16, 4), :],
        6: column_ref[2 * odd_x, pl.ds(16, 4), :],
    }
    near = column_ref[1, pl.ds(16, 4), :].astype(jnp.int32)
    core = [center_ref[:, r * LANES : (r + 1) * LANES] for r in range(4)]
    asked = (
        ghost_slots((1, 6), listed, on_grid(grid, where_ref), ghost_ref),
        jnp.concatenate([jnp.where(near < OWNED, near, -1)] + core, axis=0),
    )
    for g, slot in enumerate(asked):
        early_slot_ref[pl.ds(8 * g, 8), :] = slot
        for c, found in enumerate(kept_values(slot, kept_ref)):
            early_ref[g, c] = found


def arrange(ix, iy, own_ref, even_ref, odd_ref, grid_ref):
    odd_x, odd_y = ix & 1, iy & 1
    for dx in (-1, 0, 1):
        block = {-1: 2 - 2 * odd_x, 0: 1, 1: 2 * odd_x}[dx]
        even, odd = even_ref[block], odd_ref[block]
        grid_ref[0, dx + 1] = jnp.where(odd_y > 0, even, odd)
        grid_ref[1, dx + 1] = own_ref[block]
        grid_ref[2, dx + 1] = jnp.where(odd_y > 0, odd, even)


def answer_kernel(
    grid, where_ref, own_ref, even_ref, odd_ref, ghost_ref, kept_ref, early_ref, early_slot_ref,
    to_even_ref, to_odd_ref, same_ref, center_out, slot_ref, arrive_ref, grid_ref,
):
    ix, iy = where_ref[0], where_ref[1]
    arrange(ix, iy, own_ref, even_ref, odd_ref, grid_ref)
    inside = on_grid(grid, where_ref)
    listed = []
    for k, (dx, dy) in enumerate(DIRS):
        listed.append(grid_ref[dy + 1, dx + 1, pl.ds(16, 4), :])
        for p in range(2):
            row = grid_ref[dy + 1, dx + 1, pl.ds(8 * p + 7 - k, 1), :]
            arrive_ref[p, pl.ds(k, 1), :] = row * inside[k].astype(F32)
    values = {}
    for pair in ((1, 6), (8, 9), (0, 2), (5, 7), (3, 4)):
        if pair in ((1, 6), (8, 9)):
            g = 0 if pair == (1, 6) else 1
            slot = early_slot_ref[pl.ds(8 * g, 8), :]
            found = [early_ref[g, c] for c in range(4)]
        else:
            slot = ghost_slots(pair, listed, inside, ghost_ref)
            found = kept_values(slot, kept_ref)
        found = late_values(slot, arrive_ref, found)
        for half, d in enumerate(pair):
            rows = slice(4 * half, 4 * half + 4)
            slot_ref[pl.ds(4 * d, 4), :] = slot[rows, :]
            values[d] = [found[c][rows, :] for c in range(4)]
    flip = (ix & 1) > 0
    for c in range(4):
        rows = pl.ds(4 * c, 4)
        center_out[rows, :] = values[9][c]
        for y, (lower, mid, upper) in enumerate(((0, 3, 5), (1, 8, 6), (2, 4, 7))):
            same_ref[y, rows, :] = values[mid][c]
            to_even_ref[y, rows, :] = jnp.where(flip, values[lower][c], values[upper][c])
            to_odd_ref[y, rows, :] = jnp.where(flip, values[upper][c], values[lower][c])


def edge_kernel(
    layers,
    blocks_ref, same_ref, below_ref, above_ref, center_ref, core_row_ref,
    w_rad_ref, w_kc_ref, w_kn_ref, w_two_ref, w_edge_t_ref, w_env_t_ref, w_up_ref, w_out_ref,
    msg_ref,
    lhs_ref, rhs_ref, back_ref, joined_ref, latent_ref, d_latent_ref, edge_mix_ref, env_mix_ref,
    pooled_ref, act_ref, slope_ref,
):
    near = same_ref[1] + below_ref[...] + above_ref[...]
    mid = center_ref[...]

    def flat(rows, c):
        return jnp.concatenate([rows[4 * c + r : 4 * c + r + 1, :] for r in range(4)], axis=1)

    delta = [flat(near, c) - flat(mid, c) for c in range(3)]
    kind_n, kind_c = flat(near, 3), flat(mid, 3)
    radius = jnp.sqrt(delta[0] * delta[0] + delta[1] * delta[1] + delta[2] * delta[2] + SOFTENING)
    inv_radius = 1.0 / radius
    block = lax.broadcasted_iota(jnp.int32, (1, EDGES), 1) >> 7
    live = (block < blocks_ref[0]) & (kind_c > 0.5) & (kind_n > 0.5)
    live = jnp.where(live, 1.0, 0.0)
    ramp = jnp.maximum(0.0, 1.0 - radius * radius / (CUTOFF * CUTOFF))
    envelope = live * ramp * ramp
    ux, uy, uz = (d * (1.0 / CUTOFF) for d in delta)
    sph = [
        ROOT3 * ux,
        ROOT3 * uy,
        ROOT3 * uz,
        ROOT15 * ux * uy,
        ROOT15 * uy * uz,
        ROOT15 * ux * uz,
        (0.5 * ROOT5) * (2.0 * uz * uz - ux * ux - uy * uy),
        (0.5 * ROOT15) * (ux * ux - uy * uy),
    ]
    q8 = lax.broadcasted_iota(jnp.int32, (8, EDGES), 0)
    shift = radius - q8.astype(F32) * (CUTOFF / 7.0)
    radial = jnp.exp(-(shift * shift) * (1.0 / (BASIS_WIDTH * BASIS_WIDTH)))
    ids = (q8 & 3) + 1
    kinds = jnp.where(q8 < 4, kind_c, kind_n)
    onehot = jnp.where(kinds == ids.astype(F32), 1.0, 0.0)
    core_row = core_row_ref[...].astype(F32)
    same_center = column_of(core_row) == core_row
    zero_row = jnp.zeros((1, EDGES), F32)

    together = jnp.where(same_center, 1.0, 0.0).astype(BF16)

    def gram(rows):
        top, rest = [], []
        for row in rows:
            a, b = split(row)
            top.append(a.astype(F32))
            rest.append(b.astype(F32))
        fill = [jnp.zeros((LANES - 3 * len(rows), EDGES), F32)]
        a = jnp.concatenate(top + top + rest + fill, axis=0).astype(BF16)
        b = jnp.concatenate(top + rest + top + fill, axis=0).astype(BF16)
        return mm(a, b, TN).astype(BF16) * together

    grams = [together, gram(sph[:3]), gram(sph[3:])]

    w_top, w_rest = halves(
        jnp.concatenate([w_rad_ref[...], w_kc_ref[...], w_kn_ref[...]], axis=0)
    )
    f_top, f_rest = halves(jnp.concatenate([radial, onehot], axis=0))
    w_in = jnp.concatenate([w_top, w_rest, w_top, jnp.zeros((LANES - 48, 256), F32)], axis=0)
    feats = jnp.concatenate([f_top, f_top, f_rest, jnp.zeros((LANES - 48, EDGES), F32)], axis=0)
    pre = mm(w_in.astype(BF16), feats.astype(BF16), TN)

    def sigmoid(x):
        return 0.5 * jnp.tanh(0.5 * x) + 0.5

    gate0 = sigmoid(pre)
    hidden = (pre * gate0).astype(BF16)
    slope0 = gate0 * (1.0 + pre * (1.0 - gate0))
    two = mm(w_two_ref[...], hidden, TN)
    gate1 = sigmoid(two)
    act1 = two * gate1
    slope1 = gate1 * (1.0 + two * (1.0 - gate1))
    latent_ref[...] = act1 * envelope

    def forward(t, carry):
        latent = latent_ref[...]
        latent_b = latent.astype(BF16)
        edge_mix = mm(w_edge_t_ref[t], latent_b)
        env_mix = mm(w_env_t_ref[t], latent_b).astype(BF16)
        pooled = jnp.concatenate(
            [mm(env_mix[64 * l : 64 * l + 64, :], grams[l]) for l in range(3)], axis=0
        ) * ENV_SCALE
        invariants = (edge_mix * pooled).astype(BF16)
        update = mm(w_up_ref[t], jnp.concatenate([latent_b, invariants], axis=0), TN)
        gate = sigmoid(update)
        act = update * gate
        edge_mix_ref[t] = edge_mix
        env_mix_ref[t] = env_mix
        pooled_ref[t] = pooled
        act_ref[t] = act
        slope_ref[t] = gate * (1.0 + update * (1.0 - gate))
        latent_ref[...] = latent + act * envelope
        return carry

    lax.fori_loop(0, layers, forward, 0)
    w_out = column_of(w_out_ref[...].astype(F32))
    read = jnp.sum(latent_ref[...].astype(BF16).astype(F32) * w_out, axis=0, keepdims=True)
    energy = envelope * read
    d_latent_ref[...] = (w_out * envelope).astype(BF16).astype(F32)

    def backward(s, d_env):
        t = layers - 1 - s
        d_latent = d_latent_ref[...]
        d_env = d_env + jnp.sum(d_latent * act_ref[t], axis=0, keepdims=True)
        d_update = (d_latent * envelope * slope_ref[t]).astype(BF16)
        joined_ref[...] = mm(w_up_ref[t], d_update)
        d_inv = joined_ref[pl.ds(256, 192), :]
        d_edge_mix = (d_inv * pooled_ref[t]).astype(BF16)
        d_pooled = (d_inv * edge_mix_ref[t] * ENV_SCALE).astype(BF16)
        d_env_mix = jnp.concatenate(
            [mm(d_pooled[64 * l : 64 * l + 64, :], grams[l]) for l in range(3)], axis=0
        ).astype(BF16)
        for l in range(1, 3):
            mix_l = env_mix_ref[t, pl.ds(64 * l, 64), :]
            pool_l = d_pooled[64 * l : 64 * l + 64, :]
            lhs_ref[l - 1, t] = jnp.concatenate([pool_l, mix_l], axis=0)
            rhs_ref[l - 1, t] = jnp.concatenate([mix_l, pool_l], axis=0)
        back_ref[...] = mm(
            jnp.concatenate([w_edge_t_ref[t], w_env_t_ref[t]], axis=0),
            jnp.concatenate([d_edge_mix, d_env_mix], axis=0),
            TN,
        )
        d_latent_ref[...] = d_latent + joined_ref[pl.ds(0, 256), :] + back_ref[...]
        return d_env

    d_env = lax.fori_loop(0, layers, backward, read)
    d_latent = d_latent_ref[...]
    d_env = d_env + jnp.sum(d_latent * act1, axis=0, keepdims=True)
    d_two = (d_latent * envelope * slope1).astype(BF16)
    d_pre = mm(w_two_ref[...], d_two) * slope0
    w_back = jnp.concatenate([w_top[:8, :], w_rest[:8, :]], axis=0).astype(BF16)
    d_radial = mm(w_back, d_pre.astype(BF16))
    d_radial = d_radial[:8, :] + d_radial[8:, :]
    d_radius = jnp.sum(
        d_radial * radial * shift, axis=0, keepdims=True
    ) * (-2.0 / (BASIS_WIDTH * BASIS_WIDTH))
    d_radius = d_radius - d_env * live * ramp * radius * (4.0 / (CUTOFF * CUTOFF))

    def both(ref, l):
        return jnp.concatenate([ref[l - 1, t] for t in range(layers)], axis=0)

    d_sph = []
    for l, rows in ((1, sph[:3]), (2, sph[3:])):
        pairs = mm(both(lhs_ref, l), both(rhs_ref, l), TN).astype(BF16) * together
        fill = [zero_row] * (8 - len(rows))
        y_top, y_rest = halves(jnp.concatenate(list(rows) + fill, axis=0))
        got = mm(jnp.concatenate([y_top, y_rest], axis=0).astype(BF16), pairs)
        got = got[:8, :] + got[8:, :]
        d_sph += [got[i : i + 1, :] for i in range(len(rows))]
    d1, d2, d3, d4, d5, d6, d7, d8 = d_sph
    du = [
        ROOT3 * d1 + ROOT15 * (uy * d4 + uz * d6 + ux * d8) - ROOT5 * ux * d7,
        ROOT3 * d2 + ROOT15 * (ux * d4 + uz * d5 - uy * d8) - ROOT5 * uy * d7,
        ROOT3 * d3 + ROOT15 * (uy * d5 + ux * d6) + (2.0 * ROOT5) * uz * d7,
    ]
    scale = d_radius * inv_radius
    for c in range(3):
        grad = scale * delta[c] + du[c] * (1.0 / CUTOFF)
        for r in range(4):
            msg_ref[pl.ds(4 * c + r, 1), :] = grad[:, r * LANES : (r + 1) * LANES]
    for r in range(4):
        msg_ref[pl.ds(12 + r, 1), :] = energy[:, r * LANES : (r + 1) * LANES]


def spread(entries, chans):
    sub32 = lax.broadcasted_iota(jnp.int32, (32, LANES), 0)
    sub128 = lax.broadcasted_iota(jnp.int32, (LANES, LANES), 0)
    pieces = len(entries[0][2]) // chans
    total = jnp.zeros((pieces * chans * 32, LANES), F32)
    for first in range(0, len(entries), 2):
        a_parts, b_parts = [], []
        for high, low, values in entries[first : first + 2]:
            here = sub32 == high
            a_parts.append(jnp.concatenate([jnp.where(here, v, 0.0) for v in values], axis=0))
            b_parts.append(jnp.where(sub128 == low, 1.0, 0.0))
        a = jnp.concatenate(a_parts, axis=1).astype(BF16)
        b = jnp.concatenate(b_parts, axis=1).astype(BF16)
        total = total + mm(a, b, NT)
    tables = [total[32 * i : 32 * i + 32, :] for i in range(pieces * chans)]
    return [sum(tables[c * pieces + 1 : (c + 1) * pieces], tables[c * pieces]) for c in range(chans)]


def store_flat(ref, lead, table):
    for h in range(27):
        stop = min((h + 1) * LANES, OWNED)
        ref[lead + (slice(None), slice(h * LANES, stop))] = table[h : h + 1, : stop - h * LANES]


def ghost_entries(slot_ref, block_of, wanted):
    slots = slot_ref[pl.ds(0, 32), :]
    high, low = slots >> 7, slots & 127
    entries = []
    for o, (dx, dy) in enumerate(DIRS):
        if (dy == 0) != wanted:
            continue
        top, rest = halves(block_of(dx, dy))
        for r in range(4):
            values = []
            for c in range(3):
                row = slice(4 * c + r, 4 * c + r + 1)
                values += [top[row, :], rest[row, :]]
            row = slice(4 * o + r, 4 * o + r + 1)
            entries.append((high[row, :], low[row, :], values))
    return entries


def home_kernel(where_ref, column_ref, slot_ref, force_ref, atom_ref):
    top, rest = halves(column_ref[1])
    slots = slot_ref[pl.ds(32, 8), :]
    high, low = slots >> 7, slots & 127
    odd_x = where_ref[0] & 1

    def entry(row, values):
        return (high[row : row + 1, :], low[row : row + 1, :], values)

    def parts(c, r):
        return [top[4 * c + r : 4 * c + r + 1, :], rest[4 * c + r : 4 * c + r + 1, :]]

    def block_of(dx, dy):
        return column_ref[2 - 2 * odd_x if dx < 0 else 2 * odd_x]

    grads = [sum((parts(c, r) for c in range(3)), []) for r in range(4)]
    entries = [entry(r, [-g for g in grads[r]]) for r in range(4)]
    entries += [entry(4 + r, grads[r]) for r in range(4)]
    ghosts = [(h, l, [-v for v in values]) for h, l, values in ghost_entries(slot_ref, block_of, True)]
    for c, table in enumerate(spread(entries + ghosts, 3)):
        force_ref[c] = table
    store_flat(atom_ref, (0,), spread([entry(4 + r, parts(3, r)) for r in range(4)], 1)[0])


def return_kernel(where_ref, even_ref, odd_ref, slot_ref, force_in_ref, force_ref):
    odd_x, odd_y = where_ref[0] & 1, where_ref[1] & 1

    def block_of(dx, dy):
        block = {-1: 2 - 2 * odd_x, 0: 1, 1: 2 * odd_x}[dx]
        use_even = (odd_y > 0) if dy < 0 else (odd_y == 0)
        return jnp.where(use_even, even_ref[block], odd_ref[block])

    for c, table in enumerate(spread(ghost_entries(slot_ref, block_of, False), 3)):
        store_flat(force_ref, (c,), force_in_ref[c] - table)


def call(kernel, outs, args, smem=(), scratch=(), hbm=False):
    many = isinstance(outs, (list, tuple))
    inside = pl.BlockSpec(memory_space=pltpu.VMEM)
    scalar = pl.BlockSpec(memory_space=pltpu.SMEM)
    outside = pl.BlockSpec(memory_space=pltpu.HBM)
    return pl.pallas_call(
        kernel,
        out_shape=outs,
        in_specs=[outside if hbm else scalar if i in smem else inside for i in range(len(args))],
        out_specs=[inside] * len(outs) if many else inside,
        scratch_shapes=list(scratch),
        compiler_params=pltpu.CompilerParams(vmem_limit_bytes=WHOLE_VMEM if hbm else VMEM_LIMIT),
    )(*args)


def exchange(to_even, to_odd, axis):
    nx, ny = lax.axis_size("gx"), lax.axis_size("gy")
    even, odd = [], []
    for i in range(nx):
        for j in range(ny):
            k, count = (i, nx) if axis == "gx" else (j, ny)
            pair = k ^ 1
            other = ((k + 1) ^ 1) - 1
            ends = other < 0 or other >= count
            if axis == "gx":
                to = (pair, j)
                far = (i, j ^ 1) if ends else (other, j)
            else:
                to = (i, pair)
                far = (i ^ 1, j) if ends else (i, other)
            even.append((i * ny + j, to[0] * ny + to[1]))
            odd.append((i * ny + j, far[0] * ny + far[1]))
    axes = ("gx", "gy")
    b = lax.optimization_barrier((lax.ppermute(to_odd, axes, odd), lax.ppermute(to_even, axes, even)))
    return b[1], b[0]


def shaped(*dims, dtype=F32):
    return jax.ShapeDtypeStruct(dims, dtype)


def edge_call(layers, args):
    return call(
        lambda *refs: edge_kernel(layers, *refs),
        shaped(16, LANES),
        args,
        smem=(0,),
        scratch=(
            pltpu.VMEM((2, layers, 128, EDGES), BF16),
            pltpu.VMEM((2, layers, 128, EDGES), BF16),
            pltpu.VMEM((256, EDGES), F32),
            pltpu.VMEM((448, EDGES), F32),
            pltpu.VMEM((256, EDGES), F32),
            pltpu.VMEM((256, EDGES), F32),
            pltpu.VMEM((layers, 192, EDGES), F32),
            pltpu.VMEM((layers, 192, EDGES), BF16),
            pltpu.VMEM((layers, 192, EDGES), F32),
            pltpu.VMEM((layers, 256, EDGES), F32),
            pltpu.VMEM((layers, 256, EDGES), F32),
        ),
    )


def per_device(
    positions,
    species,
    mig_rows,
    ghost_rows,
    edge_center,
    edge_neighbor,
    edge_blocks,
    w_radial,
    w_kind_center,
    w_kind_neigh,
    w_two,
    w_edge,
    w_env,
    w_update,
    w_out,
):
    layers = w_edge.shape[0]
    pos = positions.reshape(3, 1, SLOTS)
    kind = species.reshape(1, SLOTS)
    mig = mig_rows.reshape(8, MOVES)
    ghosts = ghost_rows.reshape(8, GHOSTS)
    centers = edge_center.reshape(1, EDGES)
    nbrs = edge_neighbor.reshape(1, EDGES)
    blocks = edge_blocks.reshape(1)
    grid = (lax.axis_size("gx"), lax.axis_size("gy"))
    place = jnp.stack([lax.axis_index("gx"), lax.axis_index("gy")]).astype(jnp.int32)

    odd_y = (place[1] & 1) > 0

    msg = call(
        send_kernel,
        shaped(24, LANES),
        (pos, kind, mig, nbrs),
        hbm=True,
        scratch=(
            pltpu.VMEM((3, 1, SLOTS), F32),
            pltpu.VMEM((1, SLOTS), jnp.int32),
            pltpu.VMEM((8, MOVES), jnp.int32),
            pltpu.VMEM((1, EDGES), jnp.int32),
            pltpu.SemaphoreType.DMA((4,)),
        ),
    )
    even, odd = exchange(msg, msg, "gx")
    column = jnp.stack([even, msg, odd])
    kept, early, early_slots = call(
        lambda *refs: keep_kernel(grid, *refs),
        (
            shaped(4, 24, LANES),
            shaped(2, 4, 8, LANES),
            shaped(16, LANES, dtype=jnp.int32),
        ),
        (place, pos, kind, mig, column, ghosts, centers),
        smem=(0,),
    )
    even, odd = exchange(column, column, "gy")

    to_even, to_odd, same, mids, slots, arrived = call(
        lambda *refs: answer_kernel(grid, *refs),
        (
            shaped(3, 16, LANES),
            shaped(3, 16, LANES),
            shaped(3, 16, LANES),
            shaped(16, LANES),
            shaped(40, LANES, dtype=jnp.int32),
            shaped(2, 8, LANES),
        ),
        (place, column, even, odd, ghosts, kept, early, early_slots),
        smem=(0,),
        scratch=(pltpu.VMEM((3, 3, 24, LANES), F32),),
    )
    even, odd = exchange(to_even, to_odd, "gx")

    stay = kept[:3].reshape(3, 24 * LANES)[:, :SLOTS]
    late = arrived.reshape(2, 8, 2, MOVES).transpose(0, 2, 1, 3).reshape(4, 8 * MOVES)[:3]
    owned_positions = jnp.concatenate([stay, late], 1).reshape(3, 1, 1, OWNED)

    same = same + even + odd
    down, up = same[0], same[2]
    even, odd = exchange(jnp.where(odd_y, down, up), jnp.where(odd_y, up, down), "gy")

    mids, owned_positions = lax.optimization_barrier((mids, owned_positions))
    grad = edge_call(
        layers,
        (
            blocks, same, even, odd, mids, centers,
            w_radial, w_kind_center, w_kind_neigh, w_two,
            w_edge.transpose(0, 2, 1), w_env.transpose(0, 2, 1), w_update,
            w_out.reshape(1, -1),
        ),
    )
    even, odd = exchange(grad, grad, "gx")
    column = jnp.stack([even, grad, odd])
    force_home, atoms = call(
        home_kernel, (shaped(3, 32, LANES), shaped(1, 1, OWNED)), (place, column, slots), smem=(0,)
    )
    even, odd = exchange(column, column, "gy")
    forces = call(
        return_kernel, shaped(3, 1, OWNED), (place, even, odd, slots, force_home), smem=(0,)
    )
    return (owned_positions, forces.reshape(3, 1, 1, OWNED), atoms)


def solution(mesh):
    placed = (
        P(None, "gx", "gy", None),
        P("gx", "gy", None),
        P("gx", "gy", None, None),
        P("gx", "gy", None, None),
        P("gx", "gy", None),
        P("gx", "gy", None),
        P("gx", "gy"),
        P(),
        P(),
        P(),
        P(),
        P(),
        P(),
        P(),
        P(),
    )
    return jax.shard_map(
        per_device,
        mesh=mesh,
        in_specs=placed,
        out_specs=(P(None, "gx", "gy", None), P(None, "gx", "gy", None), P("gx", "gy", None)),
        check_vma=False,
    )
```
